32 devices in a mesh: rep: 4 (over z), exp: 8 (over y, x, core).
Axes of the slice: x: 2, y: 2, z: 4, core: 2. Of those that a mesh axis runs over, the one named last changes fastest.
Arguments:
- activations: bfloat16 [4096, 4096], P(('rep', 'exp')), may hold values from -6 to 6
- grad_hidden: bfloat16 [4096, 1024], P(('rep', 'exp')), may hold values from -6 to 6
- pre_gate: bfloat16 [4096, 1024], P(('rep', 'exp')), may hold values from -12 to 12
- pre_up: bfloat16 [4096, 1024], P(('rep', 'exp')), may hold values from -6 to 6
- modality: int32 [4096], P(('rep', 'exp')), may hold values from 0 to 1, as said below
- expert_index: int32 [4096], P(('rep', 'exp')), may hold values from 0 to 1
- master: float32 [16384, 2048], P(('exp', 'rep')), may hold values from -0.09375 to 0.09375
- first_moment: float32 [16384, 2048], P(('exp', 'rep')), may hold values from -18 to 18
- second_moment: float32 [16384, 2048], P(('exp', 'rep')), may hold values from 200 to 2000
Outputs:
- input_grad: bfloat16 [4096, 4096], P(('rep', 'exp'))
- new_master: float32 [16384, 2048], P(('exp', 'rep'))
- new_first: float32 [16384, 2048], P(('exp', 'rep'))
- new_second: float32 [16384, 2048], P(('exp', 'rep'))
The draws below stay inside these ranges and needn't reach their ends.
Inputs may be any that keep to these rules, and one draw needn't show every extreme that they name: Among the 128 tokens of one device no expert 2 * modality + expert_index is named more than 48 times; in every replica group of 1024 tokens one expert is named exactly 48 times on every device.
All inputs are finite; a program needn't handle non-finite values.
Results may differ from the reference program's by a relative error of at most 0.019.
Values may be sent and summed in bfloat16 or wider, within the bound.
A program may use at most 128 MiB of HBM per device.

```python
import math
import jax
import jax.numpy as jnp

D = 4096
H = 1024
EXPERTS = 4
TOK_DEV = 128
CAP = 48
GROUP_ROWS = 1024
TOKENS = 4096


def route_table(key):
    key = jax.random.fold_in(key, 11)
    blocks = TOKENS // TOK_DEV
    per_group = GROUP_ROWS // TOK_DEV
    key_heavy, key_blocks = jax.random.split(key, 2)
    heavy = jax.random.randint(key_heavy, (TOKENS // GROUP_ROWS,), 0, EXPERTS).astype(jnp.int32)
    heavy_block = jnp.repeat(heavy, per_group, total_repeat_length=blocks)

    def one_block(block_key, top):
        key_pool, key_order = jax.random.split(block_key, 2)
        pool = (jax.random.permutation(key_pool, (EXPERTS - 1) * CAP)[:TOK_DEV - CAP] // CAP).astype(jnp.int32)
        others = pool + (pool >= top).astype(jnp.int32)
        filled = jnp.concatenate([jnp.full((CAP,), top, jnp.int32), others])
        return filled[jax.random.permutation(key_order, TOK_DEV)]
    table = jax.vmap(one_block)(jax.random.split(key_blocks, blocks), heavy_block)
    return table.reshape(TOKENS).astype(jnp.int32)


def draw_modality(key, part):
    return (route_table(key) // (EXPERTS // 2)).astype(jnp.int32)


def draw_expert_index(key, part):
    return (route_table(key) % (EXPERTS // 2)).astype(jnp.int32)


def shard_levels(key, shape, cuts, least, largest):
    def one(axis_at, blocks):
        steps = jax.random.uniform(jax.random.fold_in(jax.random.fold_in(key, 6), axis_at), (blocks,), jnp.float32, least / len(cuts), largest / len(cuts))
        return jnp.repeat(jnp.exp(steps), shape[axis_at] // blocks).reshape((-1,) + (1,) * (len(shape) - axis_at - 1))

    gain = one(*cuts[0])
    for cut in cuts[1:]:
        gain = gain * one(*cut)
    return gain


def gaussian(key, extent, width, bound, shards=(), dtype=jnp.bfloat16):
    loudness = shard_levels(key, extent, shards, -0.22, 0.18) if shards else 1.0
    entries = jax.random.normal(key, extent, jnp.float32) * width * loudness
    return jnp.minimum(jnp.maximum(entries, -bound), bound).astype(dtype)


def setup_inputs(seed: int = 0) -> dict:
    streams_of = jax.random.split(jax.random.key(seed), 10)
    activations = gaussian(streams_of[0], (TOKENS, D), 1.0, 6.0, ((0, 32),))
    grad_hidden = gaussian(streams_of[1], (TOKENS, H), 1.0, 6.0, ((0, 32),))
    pre_gate = gaussian(streams_of[2], (TOKENS, H), 2.0, 12.0, ((0, 32),))
    pre_up = gaussian(streams_of[3], (TOKENS, H), 1.0, 6.0, ((0, 32),))
    modality = draw_modality(jax.random.fold_in(streams_of[9], 71), 0)
    expert_index = draw_expert_index(jax.random.fold_in(streams_of[9], 71), 0)
    master = gaussian(streams_of[6], (EXPERTS * D, 2 * H), D ** -0.5, 0.09375, ((0, 32),), jnp.float32)
    first_moment = gaussian(streams_of[7], (EXPERTS * D, 2 * H), 3.0, 18.0, ((0, 32),), jnp.float32)
    second_moment = jnp.clip(jnp.exp(math.log(2000.0) - 2.3025851 * jax.random.uniform(streams_of[8], (EXPERTS * D, 2 * H), jnp.float32) ** shard_levels(streams_of[8], (EXPERTS * D, 2 * H), ((0, 32),), -0.2, 0.2)), 200.0, 2000.0)
    return {"activations": activations, "grad_hidden": grad_hidden, "pre_gate": pre_gate, "pre_up": pre_up, "modality": modality, "expert_index": expert_index, "master": master, "first_moment": first_moment, "second_moment": second_moment}


beta_one = 0.9
beta_two = 0.999
learn_rate = 0.02
adam_eps = 1e-08
adam_count = 1000

def reference(activations, grad_hidden, pre_gate, pre_up, modality, expert_index, master, first_moment, second_moment):
    expert = (2 * modality + expert_index).astype(jnp.int32)
    gate_val = pre_gate.astype(jnp.float32)
    up_val = pre_up.astype(jnp.float32)
    grad_val = grad_hidden.astype(jnp.float32)
    sig = 1.0 / (1.0 + jnp.exp(-gate_val))
    grad_gate = (grad_val * up_val * sig * (1.0 + gate_val * (1.0 - sig))).astype(jnp.bfloat16)
    grad_up = (grad_val * gate_val * sig).astype(jnp.bfloat16)
    both_grads = jnp.concatenate([grad_gate, grad_up], axis=1)
    weights = master.astype(jnp.bfloat16).reshape(EXPERTS, D, 2 * H)
    input_acc = jnp.zeros((activations.shape[0], D), jnp.float32)
    grad_list = []
    for which in range(EXPERTS):
        chosen = (expert == which)[:, None]
        masked = jnp.where(chosen, both_grads, jnp.zeros_like(both_grads))
        input_acc = input_acc + jnp.dot(masked, weights[which].T, preferred_element_type=jnp.float32)
        grad_list.append(jnp.dot(activations.T, masked, preferred_element_type=jnp.float32))
    input_grad = input_acc.astype(jnp.bfloat16)
    weight_grad = jnp.stack(grad_list, axis=0).reshape(EXPERTS * D, 2 * H)
    new_first = beta_one * first_moment + (1.0 - beta_one) * weight_grad
    new_second = beta_two * second_moment + (1.0 - beta_two) * weight_grad * weight_grad
    corr_one = 1.0 - beta_one ** adam_count
    corr_two = 1.0 - beta_two ** adam_count
    update = new_first / corr_one / (jnp.sqrt(new_second / corr_two) + adam_eps)
    new_master = master - learn_rate * update
    return (input_grad, new_master, new_first, new_second)
```

```python
import jax
import jax.numpy as jnp
from jax import lax
from jax.experimental import pallas as pl
from jax.experimental.pallas import tpu as pltpu
from jax.sharding import PartitionSpec as P

EXPERTS = 4
CAP = 48


beta_one = 0.9
beta_two = 0.999
learn_rate = 0.02
adam_eps = 1e-08
adam_count = 1000


def from_partner(block, axis, stride):
    count = lax.axis_size(axis)
    route = []
    for low in range(count):
        high = low | 1 << stride
        if high != low and high < count:
            route += [(low, high), (high, low)]
    return lax.ppermute(block, axis, route)


def hidden_grads(saved_rows):
    grad_val = saved_rows[:, 0].astype(jnp.float32)
    gate_val = saved_rows[:, 1].astype(jnp.float32)
    up_val = saved_rows[:, 2].astype(jnp.float32)
    sig = 1.0 / (1.0 + jnp.exp(-gate_val))
    grad_gate = (grad_val * up_val * sig * (1.0 + gate_val * (1.0 - sig))).astype(jnp.bfloat16)
    grad_up = (grad_val * gate_val * sig).astype(jnp.bfloat16)
    return jnp.stack([grad_gate, grad_up], axis=1)


def weights_move(
    activations,
    grad_hidden,
    pre_gate,
    pre_up,
    modality,
    expert_index,
    master,
    first_moment,
    second_moment,
):
    tok_count = activations.shape[0]
    width = activations.shape[1]
    hidden = grad_hidden.shape[1]
    exp_size = lax.axis_size("exp")
    group = exp_size // EXPERTS
    piece_width = width // group
    piece_hidden = hidden // group
    capacity = CAP
    rows_total = exp_size * capacity
    expert = 2 * modality + expert_index
    onehot = (expert[:, None] == jnp.arange(EXPERTS, dtype=jnp.int32)[None, :]).astype(jnp.int32)
    before = jnp.cumsum(onehot, axis=0) - onehot
    slot_pos = jnp.sum(before * onehot, axis=1)
    same_expert = expert[None, None, :] == jnp.arange(EXPERTS, dtype=jnp.int32)[:, None, None]
    same_slot = slot_pos[None, None, :] == jnp.arange(capacity, dtype=jnp.int32)[None, :, None]
    routing = (same_expert & same_slot).astype(jnp.bfloat16)
    x_split = activations.reshape(tok_count, group, piece_width)
    x_send = jnp.einsum("ect,tgd->egcd", routing, x_split, preferred_element_type=jnp.float32)
    x_send = x_send.astype(jnp.bfloat16).reshape(EXPERTS * group, capacity, piece_width)
    saved = jnp.stack([grad_hidden, pre_gate, pre_up], axis=1)
    split_saved = saved.reshape(tok_count, 3, group, piece_hidden)
    parts = jnp.einsum("ect,tsgh->egcsh", routing, split_saved, preferred_element_type=jnp.float32)
    parts = parts.astype(jnp.bfloat16).reshape(EXPERTS * group, capacity, 3 * piece_hidden)
    x_recv, h_recv = (
        lax.all_to_all(x_send, "exp", split_axis=0, concat_axis=0, tiled=True),
        lax.all_to_all(parts, "exp", split_axis=0, concat_axis=0, tiled=True),
    )
    local = hidden_grads(h_recv.reshape(rows_total, 3, piece_hidden))
    blocks = local[None]
    position = lax.axis_index("exp")
    for level in range(group.bit_length() - 1):
        partner = from_partner(blocks, "exp", level)
        upper = position // 2**level % 2 == 1
        blocks = jnp.where(
            upper,
            jnp.concatenate([partner, blocks], axis=0),
            jnp.concatenate([blocks, partner], axis=0),
        )
    grads_flat = jnp.transpose(blocks, (1, 2, 0, 3)).reshape(rows_total, 2 * hidden)
    x_rows = x_recv.reshape(rows_total, piece_width)
    shard_bf = master.astype(jnp.bfloat16)
    dx_rows = lax.dot_general(
        grads_flat,
        lax.all_gather(shard_bf, "rep", axis=0, tiled=True),
        (((1,), (1,)), ((), ())),
        preferred_element_type=jnp.float32,
    )
    dx_send = dx_rows.astype(jnp.bfloat16).reshape(exp_size, capacity, piece_width)
    back = lax.all_to_all(dx_send, "exp", split_axis=0, concat_axis=0, tiled=True)
    back = back.reshape(EXPERTS, group, capacity, piece_width)
    input_grad = jnp.einsum("ect,egcd->tgd", routing, back, preferred_element_type=jnp.float32)
    input_grad = input_grad.reshape(tok_count, width).astype(jnp.bfloat16)
    weight_grad = lax.psum_scatter(
        lax.dot_general(
            x_rows, grads_flat, (((0,), (0,)), ((), ())), preferred_element_type=jnp.float32
        ).astype(jnp.bfloat16),
        "rep",
        scatter_dimension=0,
        tiled=True,
    ).astype(jnp.float32)
    new_first = beta_one * first_moment + (1.0 - beta_one) * weight_grad
    new_second = beta_two * second_moment + (1.0 - beta_two) * weight_grad * weight_grad
    corr_one = 1.0 - beta_one**adam_count
    corr_two = 1.0 - beta_two**adam_count
    update = new_first / corr_one / (jnp.sqrt(new_second / corr_two) + adam_eps)
    new_master = master - learn_rate * update
    return (input_grad, new_master, new_first, new_second)


MESH = pl.DeviceIdType.MESH
VMEM_GRANT = 56 * 2**20


def flip(position, mask, count):
    out = 0
    bit = 1
    while bit < count:
        have = position // bit % 2
        out = out + bit * ((1 - have) if mask & bit else have)
        bit *= 2
    return out


def rows_kernel(
    x_ref, g_ref, r_ref, master_ref,
    dx_ref, wg_ref,
    gz, xz, rz, ps, rb, ph, wf, wb, xt, db, bk, us, fin,
    g_send, g_recv, x_send, x_recv, r_send, r_recv,
    p_send, p_recv, h_send, h_recv, b_send, b_recv, u_send, u_recv, w_sem,
):
    n = lax.axis_size("rep")
    q = lax.axis_size("exp")
    z = lax.axis_index("rep")
    me = lax.axis_index("exp")
    group = q // EXPERTS
    e_me = me // group
    c_me = me % group
    tok = x_ref.shape[0]
    width = x_ref.shape[1]
    piece = master_ref.shape[0]
    hid2 = master_ref.shape[1]
    half = hid2 // group
    strip = width // group
    slots = EXPERTS * CAP
    rows = q * CAP
    layers = [flip(z, k, n) for k in range(n)]

    weights = pltpu.make_async_copy(master_ref, wf, w_sem)
    weights.start()

    barrier = pltpu.get_barrier_semaphore()
    for k in range(1, n):
        pl.semaphore_signal(barrier, inc=1, device_id={"rep": layers[k]}, device_id_type=MESH)
    for j in range(1, q):
        pl.semaphore_signal(barrier, inc=1, device_id={"exp": (me + j) % q}, device_id_type=MESH)
    gz[z] = g_ref[...]
    pl.semaphore_wait(barrier, n + q - 2)

    def columns(c, layer):
        return pl.ds(pl.multiple_of(c * strip + layer * piece, piece), piece)

    def g_copy(way, step):
        block = z - step if way == 0 else z + step
        to = z + 1 if way == 0 else z - 1
        return pltpu.make_async_remote_copy(
            src_ref=gz.at[block], dst_ref=gz.at[block],
            send_sem=g_send.at[way, step], recv_sem=g_recv.at[way, step],
            device_id={"rep": to}, device_id_type=MESH,
        )

    def g_sends(way, step):
        return (z >= step) & (z < n - 1) if way == 0 else (z + step < n) & (z > 0)

    def g_lands(way, step):
        return z - 1 - step >= 0 if way == 0 else z + 1 + step < n

    def r_copy(k):
        return pltpu.make_async_remote_copy(
            src_ref=rz.at[0], dst_ref=rz.at[k], send_sem=r_send.at[k], recv_sem=r_recv.at[k],
            device_id={"rep": layers[k]}, device_id_type=MESH,
        )

    def x_copy(k, c):
        return pltpu.make_async_remote_copy(
            src_ref=x_ref.at[:, columns(c, layers[k])], dst_ref=xz.at[k, c],
            send_sem=x_send.at[k, c], recv_sem=x_recv.at[k, c],
            device_id={"rep": layers[k]}, device_id_type=MESH,
        )

    def p_copy(k, j):
        to = (me + j) % q
        return pltpu.make_async_remote_copy(
            src_ref=ps.at[k, to // group, to % group], dst_ref=rb.at[k, me],
            send_sem=p_send.at[k, j], recv_sem=p_recv.at[k, j],
            device_id={"exp": to}, device_id_type=MESH,
        )

    def h_copy(k, m):
        to = e_me * group + (c_me + group - m) % group
        return pltpu.make_async_remote_copy(
            src_ref=rb.at[k, :, :, pl.ds(0, half)], dst_ref=ph.at[m - 1, k],
            send_sem=h_send.at[k, m], recv_sem=h_recv.at[k, m],
            device_id={"exp": to}, device_id_type=MESH,
        )

    def b_copy(k, j):
        to = (me + j) % q
        return pltpu.make_async_remote_copy(
            src_ref=db.at[k, to], dst_ref=bk.at[k, c_me, e_me],
            send_sem=b_send.at[k, j], recv_sem=b_recv.at[k, j],
            device_id={"exp": to}, device_id_type=MESH,
        )

    def u_copy(k):
        return pltpu.make_async_remote_copy(
            src_ref=us.at[k], dst_ref=fin.at[k], send_sem=u_send.at[k], recv_sem=u_recv.at[k],
            device_id={"rep": layers[k]}, device_id_type=MESH,
        )

    def g_start(step):
        for way in range(2):
            @pl.when(g_sends(way, step))
            def _():
                g_copy(way, step).start()

    def g_land(step):
        for way in range(2):
            @pl.when(g_lands(way, step))
            def _():
                g_copy(way, step).wait_recv()

    def pack(k):
        if k:
            r_copy(k).wait_recv()
            for c in range(group):
                x_copy(k, c).wait_recv()
        route = rz[k]
        for c in range(group):
            part = jnp.dot(
                route, gz[layers[k], :, c * half : (c + 1) * half],
                preferred_element_type=jnp.float32,
            )
            ps[k, :, c, :, :half] = part.astype(jnp.bfloat16).reshape(EXPERTS, CAP, half)
            part = jnp.dot(route, xz[k, c], preferred_element_type=jnp.float32)
            ps[k, :, c, :, half:] = part.astype(jnp.bfloat16).reshape(EXPERTS, CAP, piece)
        for j in range(1, q):
            p_copy(k, j).start()
        rb[k, me] = ps[k, e_me, c_me]

    def exchange(k):
        for j in range(1, q):
            p_copy(k, j).wait_recv()
        for m in range(1, group):
            h_copy(k, m).start()
        xt[:, k * rows : (k + 1) * rows] = rb[k, :, :, half:].reshape(rows, piece).T

    def grads_of(k, m):
        if m == 0:
            return rb[k, :, :, :half].reshape(rows, half)
        return ph[m - 1, k].reshape(rows, half)

    def hidden_at(m):
        return pl.ds(pl.multiple_of((c_me + m) % group * half, half), half)

    def input_rows(k):
        total = None
        for m in range(group):
            if m:
                h_copy(k, m).wait_recv()
            part = lax.dot_general(
                grads_of(k, m), wb[:, hidden_at(m)], (((1,), (1,)), ((), ())),
                preferred_element_type=jnp.float32,
            )
            total = part if total is None else total + part
        db[k] = total.astype(jnp.bfloat16).reshape(q, CAP, piece)
        for j in range(1, q):
            b_copy(k, j).start()
        bk[k, c_me, e_me] = db[k, me]

    def unpack(k):
        for j in range(1, q):
            b_copy(k, j).wait_recv()
        for c in range(group):
            part = lax.dot_general(
                rz[k], bk[k, c].reshape(slots, piece), (((0,), (0,)), ((), ())),
                preferred_element_type=jnp.float32,
            )
            part = part.astype(jnp.bfloat16)
            if k:
                us[k, c] = part
            else:
                dx_ref[:, columns(c, z)] = part
        if k:
            u_copy(k).start()

    rz[0] = r_ref[...]
    for k in range(1, n):
        r_copy(k).start()
    g_start(0)
    for k in range(1, n):
        for c in range(group):
            x_copy(k, c).start()
    for c in range(group):
        xz[0, c] = x_ref[:, columns(c, z)]
    pack(0)
    weights.wait()
    wb[...] = wf[...].astype(jnp.bfloat16)
    for k in range(1, n + 4):
        if k < n:
            g_land(k - 1)
            if k < n - 1:
                g_start(k)
            pack(k)
        if 0 <= k - 1 < n:
            exchange(k - 1)
        if 0 <= k - 2 < n:
            input_rows(k - 2)
        if k == n + 1:
            for m in range(group):
                for k2 in range(0, half, 256):
                    acc = None
                    for b in range(n):
                        lhs = xt[:, b * rows : (b + 1) * rows]
                        if m == 0:
                            rhs = rb[b, :, :, k2 : k2 + 256]
                        else:
                            rhs = ph[m - 1, b, :, :, k2 : k2 + 256]
                        part = jnp.dot(lhs, rhs.reshape(rows, 256), preferred_element_type=jnp.float32)
                        acc = part if acc is None else acc + part
                    at = pl.multiple_of((c_me + m) % group * half + k2, 256)
                    wg_ref[:, pl.ds(at, 256)] = acc
        if 0 <= k - 4 < n:
            unpack(k - 4)
    for k in range(1, n):
        u_copy(k).wait_recv()
        for c in range(group):
            dx_ref[:, columns(c, layers[k])] = fin[k, c]

    for step in range(n - 1):
        for way in range(2):
            @pl.when(g_sends(way, step))
            def _():
                g_copy(way, step).wait_send()
    for k in range(n):
        if k:
            r_copy(k).wait_send()
            for c in range(group):
                x_copy(k, c).wait_send()
            u_copy(k).wait_send()
        for j in range(1, q):
            p_copy(k, j).wait_send()
            b_copy(k, j).wait_send()
        for m in range(1, group):
            h_copy(k, m).wait_send()


def tokens_move(
    activations,
    grad_hidden,
    pre_gate,
    pre_up,
    modality,
    expert_index,
    master,
    first_moment,
    second_moment,
):
    n = lax.axis_size("rep")
    q = lax.axis_size("exp")
    group = q // EXPERTS
    tok, width = activations.shape
    piece, hid2 = master.shape
    half = hid2 // group
    expert = 2 * modality + expert_index
    onehot = (expert[:, None] == jnp.arange(EXPERTS, dtype=jnp.int32)[None, :]).astype(jnp.int32)
    before = jnp.cumsum(onehot, axis=0) - onehot
    slot_pos = jnp.sum(before * onehot, axis=1)
    place = expert * CAP + slot_pos
    routing = place[None, :] == jnp.arange(EXPERTS * CAP, dtype=jnp.int32)[:, None]
    routing = routing.astype(jnp.bfloat16)
    grads = hidden_grads(jnp.stack([grad_hidden, pre_gate, pre_up], axis=1)).reshape(tok, hid2)
    vmem = pl.BlockSpec(memory_space=pltpu.VMEM)
    bf16 = jnp.bfloat16
    dma = pltpu.SemaphoreType.DMA
    input_grad, weight_grad = pl.pallas_call(
        rows_kernel,
        out_shape=(
            jax.ShapeDtypeStruct((tok, width), bf16),
            jax.ShapeDtypeStruct((piece, hid2), jnp.float32),
        ),
        in_specs=[vmem, vmem, vmem, pl.BlockSpec(memory_space=pl.ANY)],
        out_specs=(vmem, vmem),
        scratch_shapes=[
            pltpu.VMEM((n, tok, hid2), bf16),
            pltpu.VMEM((n, group, tok, piece), bf16),
            pltpu.VMEM((n, EXPERTS * CAP, tok), bf16),
            pltpu.VMEM((n, EXPERTS, group, CAP, half + piece), bf16),
            pltpu.VMEM((n, q, CAP, half + piece), bf16),
            pltpu.VMEM((group - 1, n, q, CAP, half), bf16),
            pltpu.VMEM((piece, hid2), jnp.float32),
            pltpu.VMEM((piece, hid2), bf16),
            pltpu.VMEM((piece, n * q * CAP), bf16),
            pltpu.VMEM((n, q, CAP, piece), bf16),
            pltpu.VMEM((n, group, EXPERTS, CAP, piece), bf16),
            pltpu.VMEM((n, group, tok, piece), bf16),
            pltpu.VMEM((n, group, tok, piece), bf16),
            dma((2, n)), dma((2, n)),
            dma((n, group)), dma((n, group)),
            dma((n,)), dma((n,)),
            dma((n, q)), dma((n, q)),
            dma((n, group)), dma((n, group)),
            dma((n, q)), dma((n, q)),
            dma((n,)), dma((n,)),
            dma,
        ],
        compiler_params=pltpu.CompilerParams(
            collective_id=0, has_side_effects=True, vmem_limit_bytes=VMEM_GRANT
        ),
        name="rows_kernel",
    )(activations, grads, routing, master)
    new_first = beta_one * first_moment + (1.0 - beta_one) * weight_grad
    new_second = beta_two * second_moment + (1.0 - beta_two) * weight_grad * weight_grad
    corr_one = 1.0 - beta_one**adam_count
    corr_two = 1.0 - beta_two**adam_count
    update = new_first / corr_one / (jnp.sqrt(new_second / corr_two) + adam_eps)
    new_master = master - learn_rate * update
    return (input_grad, new_master, new_first, new_second)


def body(*blocks):
    n = lax.axis_size("rep")
    q = lax.axis_size("exp")
    group = q // EXPERTS
    tok, width = blocks[0].shape
    piece, hid2 = blocks[6].shape
    held = n * q * CAP * (hid2 + 4 * piece) * 2 + 12 * piece * hid2
    held += n * tok * (hid2 + 3 * group * piece) * 2 + n * EXPERTS * CAP * group * hid2
    fits = held <= VMEM_GRANT * 3 // 4 and group >= 2 and n & (n - 1) == 0
    if fits and piece % 128 == 0 and hid2 // group % 256 == 0 and q * CAP % 128 == 0:
        return tokens_move(*blocks)
    return weights_move(*blocks)


def solution(mesh):
    in_specs = (
        P(("rep", "exp"), None),
        P(("rep", "exp"), None),
        P(("rep", "exp"), None),
        P(("rep", "exp"), None),
        P(("rep", "exp")),
        P(("rep", "exp")),
        P(("exp", "rep"), None),
        P(("exp", "rep"), None),
        P(("exp", "rep"), None),
    )
    out_specs = (
        P(("rep", "exp"), None),
        P(("exp", "rep"), None),
        P(("exp", "rep"), None),
        P(("exp", "rep"), None),
    )
    return jax.shard_map(body, mesh=mesh, in_specs=in_specs, out_specs=out_specs, check_vma=False)
```

```python
import jax
import jax.numpy as jnp
from jax import lax
from jax.experimental import pallas as pl
from jax.experimental.pallas import tpu as pltpu
from jax.sharding import PartitionSpec as P

EXPERTS = 4
CAP = 48


beta_one = 0.9
beta_two = 0.999
learn_rate = 0.02
adam_eps = 1e-08
adam_count = 1000


def from_partner(block, axis, stride):
    count = lax.axis_size(axis)
    route = []
    for low in range(count):
        high = low | 1 << stride
        if high != low and high < count:
            route += [(low, high), (high, low)]
    return lax.ppermute(block, axis, route)


def hidden_grads(saved_rows):
    grad_val = saved_rows[:, 0].astype(jnp.float32)
    gate_val = saved_rows[:, 1].astype(jnp.float32)
    up_val = saved_rows[:, 2].astype(jnp.float32)
    sig = 1.0 / (1.0 + jnp.exp(-gate_val))
    grad_gate = (grad_val * up_val * sig * (1.0 + gate_val * (1.0 - sig))).astype(jnp.bfloat16)
    grad_up = (grad_val * gate_val * sig).astype(jnp.bfloat16)
    return jnp.stack([grad_gate, grad_up], axis=1)


def weights_move(
    activations,
    grad_hidden,
    pre_gate,
    pre_up,
    modality,
    expert_index,
    master,
    first_moment,
    second_moment,
):
    tok_count = activations.shape[0]
    width = activations.shape[1]
    hidden = grad_hidden.shape[1]
    exp_size = lax.axis_size("exp")
    group = exp_size // EXPERTS
    piece_width = width // group
    piece_hidden = hidden // group
    capacity = CAP
    rows_total = exp_size * capacity
    expert = 2 * modality + expert_index
    onehot = (expert[:, None] == jnp.arange(EXPERTS, dtype=jnp.int32)[None, :]).astype(jnp.int32)
    before = jnp.cumsum(onehot, axis=0) - onehot
    slot_pos = jnp.sum(before * onehot, axis=1)
    same_expert = expert[None, None, :] == jnp.arange(EXPERTS, dtype=jnp.int32)[:, None, None]
    same_slot = slot_pos[None, None, :] == jnp.arange(capacity, dtype=jnp.int32)[None, :, None]
    routing = (same_expert & same_slot).astype(jnp.bfloat16)
    x_split = activations.reshape(tok_count, group, piece_width)
    x_send = jnp.einsum("ect,tgd->egcd", routing, x_split, preferred_element_type=jnp.float32)
    x_send = x_send.astype(jnp.bfloat16).reshape(EXPERTS * group, capacity, piece_width)
    saved = jnp.stack([grad_hidden, pre_gate, pre_up], axis=1)
    split_saved = saved.reshape(tok_count, 3, group, piece_hidden)
    parts = jnp.einsum("ect,tsgh->egcsh", routing, split_saved, preferred_element_type=jnp.float32)
    parts = parts.astype(jnp.bfloat16).reshape(EXPERTS * group, capacity, 3 * piece_hidden)
    x_recv, h_recv = (
        lax.all_to_all(x_send, "exp", split_axis=0, concat_axis=0, tiled=True),
        lax.all_to_all(parts, "exp", split_axis=0, concat_axis=0, tiled=True),
    )
    local = hidden_grads(h_recv.reshape(rows_total, 3, piece_hidden))
    blocks = local[None]
    position = lax.axis_index("exp")
    for level in range(group.bit_length() - 1):
        partner = from_partner(blocks, "exp", level)
        upper = position // 2**level % 2 == 1
        blocks = jnp.where(
            upper,
            jnp.concatenate([partner, blocks], axis=0),
            jnp.concatenate([blocks, partner], axis=0),
        )
    grads_flat = jnp.transpose(blocks, (1, 2, 0, 3)).reshape(rows_total, 2 * hidden)
    x_rows = x_recv.reshape(rows_total, piece_width)
    shard_bf = master.astype(jnp.bfloat16)
    dx_rows = lax.dot_general(
        grads_flat,
        lax.all_gather(shard_bf, "rep", axis=0, tiled=True),
        (((1,), (1,)), ((), ())),
        preferred_element_type=jnp.float32,
    )
    dx_send = dx_rows.astype(jnp.bfloat16).reshape(exp_size, capacity, piece_width)
    back = lax.all_to_all(dx_send, "exp", split_axis=0, concat_axis=0, tiled=True)
    back = back.reshape(EXPERTS, group, capacity, piece_width)
    input_grad = jnp.einsum("ect,egcd->tgd", routing, back, preferred_element_type=jnp.float32)
    input_grad = input_grad.reshape(tok_count, width).astype(jnp.bfloat16)
    weight_grad = lax.psum_scatter(
        lax.dot_general(
            x_rows, grads_flat, (((0,), (0,)), ((), ())), preferred_element_type=jnp.float32
        ).astype(jnp.bfloat16),
        "rep",
        scatter_dimension=0,
        tiled=True,
    ).astype(jnp.float32)
    new_first = beta_one * first_moment + (1.0 - beta_one) * weight_grad
    new_second = beta_two * second_moment + (1.0 - beta_two) * weight_grad * weight_grad
    corr_one = 1.0 - beta_one**adam_count
    corr_two = 1.0 - beta_two**adam_count
    update = new_first / corr_one / (jnp.sqrt(new_second / corr_two) + adam_eps)
    new_master = master - learn_rate * update
    return (input_grad, new_master, new_first, new_second)


MESH = pl.DeviceIdType.MESH
VMEM_GRANT = 56 * 2**20


def flip(position, mask, count):
    out = 0
    bit = 1
    while bit < count:
        have = position // bit % 2
        out = out + bit * ((1 - have) if mask & bit else have)
        bit *= 2
    return out


def rows_kernel(
    x_ref, grad_ref, gate_ref, up_ref, r_ref, master_ref,
    dx_ref, wg_ref,
    gz, xz, rz, ps, rb, qs, xb, ph, wf, wb, xt, acc_ref, db, bk, us, fin,
    g_send, g_recv, x_send, x_recv, r_send, r_recv,
    p_send, p_recv, q_send, q_recv, h_send, h_recv,
    b_send, b_recv, u_send, u_recv, own_sem, tile_sem, w_sem,
):
    n = lax.axis_size("rep")
    q = lax.axis_size("exp")
    z = lax.axis_index("rep")
    me = lax.axis_index("exp")
    group = q // EXPERTS
    e_me = me // group
    c_me = me % group
    tok = x_ref.shape[0]
    width = x_ref.shape[1]
    piece = master_ref.shape[0]
    hid2 = master_ref.shape[1]
    half = hid2 // group
    strip = width // group
    slots = EXPERTS * CAP
    rows = q * CAP
    layers = [flip(z, k, n) for k in range(n)]

    def columns(c, layer):
        return pl.ds(pl.multiple_of(c * strip + layer * piece, piece), piece)

    def own_copy(c):
        return pltpu.make_async_copy(x_ref.at[:, columns(c, z)], xz.at[0, c], own_sem.at[c])

    weights = pltpu.make_async_copy(master_ref, wf, w_sem)
    weights.start()

    barrier = pltpu.get_barrier_semaphore()
    for k in range(1, n):
        pl.semaphore_signal(barrier, inc=1, device_id={"rep": layers[k]}, device_id_type=MESH)
    for j in range(1, q):
        pl.semaphore_signal(barrier, inc=1, device_id={"exp": (me + j) % q}, device_id_type=MESH)
    for c in range(group):
        own_copy(c).start()
    hidden = grad_ref.shape[1]
    for at in range(0, hidden, 256):
        grad_val = grad_ref[:, at : at + 256].astype(jnp.float32)
        gate_val = gate_ref[:, at : at + 256].astype(jnp.float32)
        up_val = up_ref[:, at : at + 256].astype(jnp.float32)
        sig = 1.0 / (1.0 + jnp.exp(-gate_val))
        grad_gate = grad_val * up_val * sig * (1.0 + gate_val * (1.0 - sig))
        gz[z, :, at : at + 256] = grad_gate.astype(jnp.bfloat16)
        grad_up = grad_val * gate_val * sig
        gz[z, :, hidden + at : hidden + at + 256] = grad_up.astype(jnp.bfloat16)
    rz[0] = r_ref[...]
    pl.semaphore_wait(barrier, n + q - 2)

    def g_copy(way, step):
        block = z - step if way == 0 else z + step
        to = z + 1 if way == 0 else z - 1
        return pltpu.make_async_remote_copy(
            src_ref=gz.at[block], dst_ref=gz.at[block],
            send_sem=g_send.at[way, step], recv_sem=g_recv.at[way, step],
            device_id={"rep": to}, device_id_type=MESH,
        )

    def g_sends(way, step):
        return (z >= step) & (z < n - 1) if way == 0 else (z + step < n) & (z > 0)

    def g_lands(way, step):
        return z - 1 - step >= 0 if way == 0 else z + 1 + step < n

    def r_copy(k):
        return pltpu.make_async_remote_copy(
            src_ref=rz.at[0], dst_ref=rz.at[k], send_sem=r_send.at[k], recv_sem=r_recv.at[k],
            device_id={"rep": layers[k]}, device_id_type=MESH,
        )

    def x_copy(k, c):
        return pltpu.make_async_remote_copy(
            src_ref=x_ref.at[:, columns(c, layers[k])], dst_ref=xz.at[k, c],
            send_sem=x_send.at[k, c], recv_sem=x_recv.at[k, c],
            device_id={"rep": layers[k]}, device_id_type=MESH,
        )

    def p_copy(k, j):
        to = (me + j) % q
        return pltpu.make_async_remote_copy(
            src_ref=ps.at[k, to // group, to % group], dst_ref=rb.at[k, me],
            send_sem=p_send.at[k, j], recv_sem=p_recv.at[k, j],
            device_id={"exp": to}, device_id_type=MESH,
        )

    def q_copy(k, j):
        to = (me + j) % q
        return pltpu.make_async_remote_copy(
            src_ref=qs.at[k, to // group, to % group], dst_ref=xb.at[k, me],
            send_sem=q_send.at[k, j], recv_sem=q_recv.at[k, j],
            device_id={"exp": to}, device_id_type=MESH,
        )

    def h_copy(k, m):
        to = e_me * group + (c_me + group - m) % group
        return pltpu.make_async_remote_copy(
            src_ref=rb.at[k], dst_ref=ph.at[m - 1, k],
            send_sem=h_send.at[k, m], recv_sem=h_recv.at[k, m],
            device_id={"exp": to}, device_id_type=MESH,
        )

    def b_copy(k, j):
        to = (me + j) % q
        return pltpu.make_async_remote_copy(
            src_ref=db.at[k, to], dst_ref=bk.at[k, c_me, e_me],
            send_sem=b_send.at[k, j], recv_sem=b_recv.at[k, j],
            device_id={"exp": to}, device_id_type=MESH,
        )

    def u_copy(k):
        return pltpu.make_async_remote_copy(
            src_ref=us.at[k], dst_ref=fin.at[k], send_sem=u_send.at[k], recv_sem=u_recv.at[k],
            device_id={"rep": layers[k]}, device_id_type=MESH,
        )

    def g_start(step):
        for way in range(2):
            @pl.when(g_sends(way, step))
            def _():
                g_copy(way, step).start()

    def g_land(step):
        for way in range(2):
            @pl.when(g_lands(way, step))
            def _():
                g_copy(way, step).wait_recv()

    def pack(k):
        if k:
            r_copy(k).wait_recv()
        route = rz[k]
        for c in range(group):
            part = jnp.dot(
                route, gz[layers[k], :, c * half : (c + 1) * half],
                preferred_element_type=jnp.float32,
            )
            ps[k, :, c] = part.astype(jnp.bfloat16).reshape(EXPERTS, CAP, half)
        for j in range(1, q):
            p_copy(k, j).start()
        rb[k, me] = ps[k, e_me, c_me]

    def x_starts(k):
        for c in range(group):
            x_copy(k, c).start()

    def x_pack(k):
        for c in range(group):
            if k:
                x_copy(k, c).wait_recv()
            else:
                own_copy(c).wait()
            part = jnp.dot(rz[k], xz[k, c], preferred_element_type=jnp.float32)
            qs[k, :, c] = part.astype(jnp.bfloat16).reshape(EXPERTS, CAP, piece)
        for j in range(1, q):
            q_copy(k, j).start()
        xb[k, me] = qs[k, e_me, c_me]

    def x_turn(k):
        for j in range(1, q):
            q_copy(k, j).wait_recv()
        xt[:, k * rows : (k + 1) * rows] = xb[k].reshape(rows, piece).T

    def exchange(k):
        for j in range(1, q):
            p_copy(k, j).wait_recv()
        for m in range(1, group):
            h_copy(k, m).start()

    def tile_copy(m, at):
        start = pl.multiple_of((c_me + m) % group * half + at, 256)
        return pltpu.make_async_copy(
            acc_ref.at[:, m * half + at : m * half + at + 256], wg_ref.at[:, pl.ds(start, 256)],
            tile_sem.at[(m * half + at) // 256],
        )

    def weight_rows(first, last):
        for m in range(group):
            for at in range(0, half, 256):
                total = None
                for k in range(first, last):
                    lhs = xt[:, k * rows : (k + 1) * rows]
                    if m == 0:
                        rhs = rb[k, :, :, at : at + 256]
                    else:
                        rhs = ph[m - 1, k, :, :, at : at + 256]
                    part = jnp.dot(lhs, rhs.reshape(rows, 256), preferred_element_type=jnp.float32)
                    total = part if total is None else total + part
                if first:
                    total = total + acc_ref[:, m * half + at : m * half + at + 256]
                acc_ref[:, m * half + at : m * half + at + 256] = total
                if last == n:
                    tile_copy(m, at).start()

    def grads_of(k, m):
        if m == 0:
            return rb[k].reshape(rows, half)
        return ph[m - 1, k].reshape(rows, half)

    def hidden_at(m):
        return pl.ds(pl.multiple_of((c_me + m) % group * half, half), half)

    def input_rows(k):
        total = None
        for m in range(group):
            if m:
                h_copy(k, m).wait_recv()
            part = lax.dot_general(
                grads_of(k, m), wb[:, hidden_at(m)], (((1,), (1,)), ((), ())),
                preferred_element_type=jnp.float32,
            )
            total = part if total is None else total + part
        db[k] = total.astype(jnp.bfloat16).reshape(q, CAP, piece)
        for j in range(1, q):
            b_copy(k, j).start()
        bk[k, c_me, e_me] = db[k, me]

    def unpack(k):
        for j in range(1, q):
            b_copy(k, j).wait_recv()
        for c in range(group):
            part = lax.dot_general(
                rz[k], bk[k, c].reshape(slots, piece), (((0,), (0,)), ((), ())),
                preferred_element_type=jnp.float32,
            )
            part = part.astype(jnp.bfloat16)
            if k:
                us[k, c] = part
            else:
                dx_ref[:, columns(c, z)] = part
        if k:
            u_copy(k).start()

    g_start(0)
    for k in range(1, n):
        r_copy(k).start()
    pack(0)
    x_pack(0)
    weights.wait()
    wb[...] = wf[...].astype(jnp.bfloat16)
    for k in range(1, n):
        g_land(k - 1)
        if k < n - 1:
            g_start(k)
        pack(k)
        if k == n - 1:
            for later in range(max(n - 2, 1), n):
                x_starts(later)
        elif k >= 2:
            x_starts(k - 1)
        exchange(k - 1)
        if k >= 2:
            input_rows(k - 2)
    exchange(n - 1)
    input_rows(n - 2)
    input_rows(n - 1)
    for k in range(n - 1):
        unpack(k)
        if k + 1 < n - 1:
            x_pack(k + 1)
    unpack(n - 1)
    x_pack(n - 1)
    for k in range(n // 2):
        x_turn(k)
    weight_rows(0, n // 2)
    for k in range(n // 2, n):
        x_turn(k)
    weight_rows(n // 2, n)
    for k in range(1, n):
        u_copy(k).wait_recv()
        for c in range(group):
            dx_ref[:, columns(c, layers[k])] = fin[k, c]
    for m in range(group):
        for at in range(0, half, 256):
            tile_copy(m, at).wait()

    for step in range(n - 1):
        for way in range(2):
            @pl.when(g_sends(way, step))
            def _():
                g_copy(way, step).wait_send()
    for k in range(n):
        if k:
            r_copy(k).wait_send()
            for c in range(group):
                x_copy(k, c).wait_send()
            u_copy(k).wait_send()
        for j in range(1, q):
            p_copy(k, j).wait_send()
            q_copy(k, j).wait_send()
            b_copy(k, j).wait_send()
        for m in range(1, group):
            h_copy(k, m).wait_send()


def tokens_move(
    activations,
    grad_hidden,
    pre_gate,
    pre_up,
    modality,
    expert_index,
    master,
    first_moment,
    second_moment,
):
    n = lax.axis_size("rep")
    q = lax.axis_size("exp")
    group = q // EXPERTS
    tok, width = activations.shape
    piece, hid2 = master.shape
    half = hid2 // group
    expert = 2 * modality + expert_index
    onehot = (expert[:, None] == jnp.arange(EXPERTS, dtype=jnp.int32)[None, :]).astype(jnp.int32)
    before = jnp.cumsum(onehot, axis=0) - onehot
    slot_pos = jnp.sum(before * onehot, axis=1)
    place = expert * CAP + slot_pos
    routing = place[None, :] == jnp.arange(EXPERTS * CAP, dtype=jnp.int32)[:, None]
    routing = routing.astype(jnp.bfloat16)
    vmem = pl.BlockSpec(memory_space=pltpu.VMEM)
    anywhere = pl.BlockSpec(memory_space=pl.ANY)
    bf16 = jnp.bfloat16
    dma = pltpu.SemaphoreType.DMA
    input_grad, weight_grad = pl.pallas_call(
        rows_kernel,
        out_shape=(
            jax.ShapeDtypeStruct((tok, width), bf16),
            jax.ShapeDtypeStruct((piece, hid2), jnp.float32),
        ),
        in_specs=[anywhere, vmem, vmem, vmem, vmem, anywhere],
        out_specs=(vmem, anywhere),
        scratch_shapes=[
            pltpu.VMEM((n, tok, hid2), bf16),
            pltpu.VMEM((n, group, tok, piece), bf16),
            pltpu.VMEM((n, EXPERTS * CAP, tok), bf16),
            pltpu.VMEM((n, EXPERTS, group, CAP, half), bf16),
            pltpu.VMEM((n, q, CAP, half), bf16),
            pltpu.VMEM((n, EXPERTS, group, CAP, piece), bf16),
            pltpu.VMEM((n, q, CAP, piece), bf16),
            pltpu.VMEM((group - 1, n, q, CAP, half), bf16),
            pltpu.VMEM((piece, hid2), jnp.float32),
            pltpu.VMEM((piece, hid2), bf16),
            pltpu.VMEM((piece, n * q * CAP), bf16),
            pltpu.VMEM((piece, hid2), jnp.float32),
            pltpu.VMEM((n, q, CAP, piece), bf16),
            pltpu.VMEM((n, group, EXPERTS, CAP, piece), bf16),
            pltpu.VMEM((n, group, tok, piece), bf16),
            pltpu.VMEM((n, group, tok, piece), bf16),
            dma((2, n)), dma((2, n)),
            dma((n, group)), dma((n, group)),
            dma((n,)), dma((n,)),
            dma((n, q)), dma((n, q)),
            dma((n, q)), dma((n, q)),
            dma((n, group)), dma((n, group)),
            dma((n, q)), dma((n, q)),
            dma((n,)), dma((n,)),
            dma((group,)), dma((hid2 // 256,)),
            dma,
        ],
        compiler_params=pltpu.CompilerParams(
            collective_id=0, has_side_effects=True, vmem_limit_bytes=VMEM_GRANT
        ),
        name="rows_kernel",
    )(activations, grad_hidden, pre_gate, pre_up, routing, master)
    new_first = beta_one * first_moment + (1.0 - beta_one) * weight_grad
    new_second = beta_two * second_moment + (1.0 - beta_two) * weight_grad * weight_grad
    corr_one = 1.0 - beta_one**adam_count
    corr_two = 1.0 - beta_two**adam_count
    update = new_first / corr_one / (jnp.sqrt(new_second / corr_two) + adam_eps)
    new_master = master - learn_rate * update
    return (input_grad, new_master, new_first, new_second)


def body(*blocks):
    n = lax.axis_size("rep")
    q = lax.axis_size("exp")
    group = q // EXPERTS
    tok, width = blocks[0].shape
    piece, hid2 = blocks[6].shape
    held = n * q * CAP * (hid2 + 4 * piece) * 2 + 12 * piece * hid2
    held += n * tok * (hid2 + 3 * group * piece) * 2 + n * EXPERTS * CAP * group * hid2
    fits = held <= VMEM_GRANT * 3 // 4 and group >= 2 and n >= 2 and n & (n - 1) == 0
    if fits and piece % 128 == 0 and hid2 % 512 == 0 and hid2 // group % 256 == 0 and q * CAP % 128 == 0:
        return tokens_move(*blocks)
    return weights_move(*blocks)


def solution(mesh):
    in_specs = (
        P(("rep", "exp"), None),
        P(("rep", "exp"), None),
        P(("rep", "exp"), None),
        P(("rep", "exp"), None),
        P(("rep", "exp")),
        P(("rep", "exp")),
        P(("exp", "rep"), None),
        P(("exp", "rep"), None),
        P(("exp", "rep"), None),
    )
    out_specs = (
        P(("rep", "exp"), None),
        P(("exp", "rep"), None),
        P(("exp", "rep"), None),
        P(("exp", "rep"), None),
    )
    return jax.shard_map(body, mesh=mesh, in_specs=in_specs, out_specs=out_specs, check_vma=False)
```

```python
import jax
import jax.numpy as jnp
from jax import lax
from jax.experimental import pallas as pl
from jax.experimental.pallas import tpu as pltpu
from jax.sharding import PartitionSpec as P

EXPERTS = 4
CAP = 48


beta_one = 0.9
beta_two = 0.999
learn_rate = 0.02
adam_eps = 1e-08
adam_count = 1000


def from_partner(block, axis, stride):
    count = lax.axis_size(axis)
    route = []
    for low in range(count):
        high = low | 1 << stride
        if high != low and high < count:
            route += [(low, high), (high, low)]
    return lax.ppermute(block, axis, route)


def hidden_grads(saved_rows):
    grad_val = saved_rows[:, 0].astype(jnp.float32)
    gate_val = saved_rows[:, 1].astype(jnp.float32)
    up_val = saved_rows[:, 2].astype(jnp.float32)
    sig = 1.0 / (1.0 + jnp.exp(-gate_val))
    grad_gate = (grad_val * up_val * sig * (1.0 + gate_val * (1.0 - sig))).astype(jnp.bfloat16)
    grad_up = (grad_val * gate_val * sig).astype(jnp.bfloat16)
    return jnp.stack([grad_gate, grad_up], axis=1)


def weights_move(
    activations,
    grad_hidden,
    pre_gate,
    pre_up,
    modality,
    expert_index,
    master,
    first_moment,
    second_moment,
):
    tok_count = activations.shape[0]
    width = activations.shape[1]
    hidden = grad_hidden.shape[1]
    exp_size = lax.axis_size("exp")
    group = exp_size // EXPERTS
    piece_width = width // group
    piece_hidden = hidden // group
    capacity = CAP
    rows_total = exp_size * capacity
    expert = 2 * modality + expert_index
    onehot = (expert[:, None] == jnp.arange(EXPERTS, dtype=jnp.int32)[None, :]).astype(jnp.int32)
    before = jnp.cumsum(onehot, axis=0) - onehot
    slot_pos = jnp.sum(before * onehot, axis=1)
    same_expert = expert[None, None, :] == jnp.arange(EXPERTS, dtype=jnp.int32)[:, None, None]
    same_slot = slot_pos[None, None, :] == jnp.arange(capacity, dtype=jnp.int32)[None, :, None]
    routing = (same_expert & same_slot).astype(jnp.bfloat16)
    x_split = activations.reshape(tok_count, group, piece_width)
    x_send = jnp.einsum("ect,tgd->egcd", routing, x_split, preferred_element_type=jnp.float32)
    x_send = x_send.astype(jnp.bfloat16).reshape(EXPERTS * group, capacity, piece_width)
    saved = jnp.stack([grad_hidden, pre_gate, pre_up], axis=1)
    split_saved = saved.reshape(tok_count, 3, group, piece_hidden)
    parts = jnp.einsum("ect,tsgh->egcsh", routing, split_saved, preferred_element_type=jnp.float32)
    parts = parts.astype(jnp.bfloat16).reshape(EXPERTS * group, capacity, 3 * piece_hidden)
    x_recv, h_recv = (
        lax.all_to_all(x_send, "exp", split_axis=0, concat_axis=0, tiled=True),
        lax.all_to_all(parts, "exp", split_axis=0, concat_axis=0, tiled=True),
    )
    local = hidden_grads(h_recv.reshape(rows_total, 3, piece_hidden))
    blocks = local[None]
    position = lax.axis_index("exp")
    for level in range(group.bit_length() - 1):
        partner = from_partner(blocks, "exp", level)
        upper = position // 2**level % 2 == 1
        blocks = jnp.where(
            upper,
            jnp.concatenate([partner, blocks], axis=0),
            jnp.concatenate([blocks, partner], axis=0),
        )
    grads_flat = jnp.transpose(blocks, (1, 2, 0, 3)).reshape(rows_total, 2 * hidden)
    x_rows = x_recv.reshape(rows_total, piece_width)
    shard_bf = master.astype(jnp.bfloat16)
    dx_rows = lax.dot_general(
        grads_flat,
        lax.all_gather(shard_bf, "rep", axis=0, tiled=True),
        (((1,), (1,)), ((), ())),
        preferred_element_type=jnp.float32,
    )
    dx_send = dx_rows.astype(jnp.bfloat16).reshape(exp_size, capacity, piece_width)
    back = lax.all_to_all(dx_send, "exp", split_axis=0, concat_axis=0, tiled=True)
    back = back.reshape(EXPERTS, group, capacity, piece_width)
    input_grad = jnp.einsum("ect,egcd->tgd", routing, back, preferred_element_type=jnp.float32)
    input_grad = input_grad.reshape(tok_count, width).astype(jnp.bfloat16)
    weight_grad = lax.psum_scatter(
        lax.dot_general(
            x_rows, grads_flat, (((0,), (0,)), ((), ())), preferred_element_type=jnp.float32
        ).astype(jnp.bfloat16),
        "rep",
        scatter_dimension=0,
        tiled=True,
    ).astype(jnp.float32)
    new_first = beta_one * first_moment + (1.0 - beta_one) * weight_grad
    new_second = beta_two * second_moment + (1.0 - beta_two) * weight_grad * weight_grad
    corr_one = 1.0 - beta_one**adam_count
    corr_two = 1.0 - beta_two**adam_count
    update = new_first / corr_one / (jnp.sqrt(new_second / corr_two) + adam_eps)
    new_master = master - learn_rate * update
    return (input_grad, new_master, new_first, new_second)


MESH = pl.DeviceIdType.MESH
VMEM_GRANT = 38 * 2**20


def flip(position, mask, count):
    out = 0
    bit = 1
    while bit < count:
        have = position // bit % 2
        out = out + bit * ((1 - have) if mask & bit else have)
        bit *= 2
    return out


def rows_kernel(
    x_ref, grad_ref, gate_ref, up_ref, r_ref, master_ref,
    dx_ref, wg_ref,
    gz, xz, rz, ps, rb, qs, xb, ph, wf, wb, xt, db, bk, us, fin,
    g_send, g_recv, x_send, x_recv, r_send, r_recv,
    p_send, p_recv, q_send, q_recv, h_send, h_recv,
    b_send, b_recv, u_send, u_recv, own_sem, tile_sem, w_sem,
):
    n = lax.axis_size("rep")
    q = lax.axis_size("exp")
    z = lax.axis_index("rep")
    me = lax.axis_index("exp")
    group = q // EXPERTS
    e_me = me // group
    c_me = me % group
    tok = x_ref.shape[0]
    width = x_ref.shape[1]
    piece = master_ref.shape[0]
    hid2 = master_ref.shape[1]
    half = hid2 // group
    strip = width // group
    slots = EXPERTS * CAP
    rows = q * CAP
    layers = [flip(z, k, n) for k in range(n)]

    def columns(c, layer):
        return pl.ds(pl.multiple_of(c * strip + layer * piece, piece), piece)

    def own_copy(c):
        return pltpu.make_async_copy(x_ref.at[:, columns(c, z)], xz.at[0, c], own_sem.at[c])

    weights = pltpu.make_async_copy(master_ref, wf, w_sem)
    weights.start()

    barrier = pltpu.get_barrier_semaphore()
    for k in range(1, n):
        pl.semaphore_signal(barrier, inc=1, device_id={"rep": layers[k]}, device_id_type=MESH)
    for j in range(1, q):
        pl.semaphore_signal(barrier, inc=1, device_id={"exp": (me + j) % q}, device_id_type=MESH)
    for c in range(group):
        own_copy(c).start()
    hidden = grad_ref.shape[1]
    for at in range(0, hidden, 256):
        grad_val = grad_ref[:, at : at + 256].astype(jnp.float32)
        gate_val = gate_ref[:, at : at + 256].astype(jnp.float32)
        up_val = up_ref[:, at : at + 256].astype(jnp.float32)
        sig = 1.0 / (1.0 + jnp.exp(-gate_val))
        grad_gate = grad_val * up_val * sig * (1.0 + gate_val * (1.0 - sig))
        gz[z, :, at : at + 256] = grad_gate.astype(jnp.bfloat16)
        grad_up = grad_val * gate_val * sig
        gz[z, :, hidden + at : hidden + at + 256] = grad_up.astype(jnp.bfloat16)
    rz[0] = r_ref[...]
    pl.semaphore_wait(barrier, n + q - 2)

    def hidden_at(m):
        return pl.ds(pl.multiple_of((c_me + m) % group * half, half), half)

    def g_copy(way, step, m):
        block = z - step if way == 0 else z + step
        to = z + 1 if way == 0 else z - 1
        return pltpu.make_async_remote_copy(
            src_ref=gz.at[block, :, hidden_at(m)], dst_ref=gz.at[block, :, hidden_at(m)],
            send_sem=g_send.at[way, step, m], recv_sem=g_recv.at[way, step, m],
            device_id={"rep": to}, device_id_type=MESH,
        )

    def g_sends(way, step):
        return (z >= step) & (z < n - 1) if way == 0 else (z + step < n) & (z > 0)

    def g_lands(way, step):
        return z - 1 - step >= 0 if way == 0 else z + 1 + step < n

    def r_copy(k):
        return pltpu.make_async_remote_copy(
            src_ref=rz.at[0], dst_ref=rz.at[k], send_sem=r_send.at[k], recv_sem=r_recv.at[k],
            device_id={"rep": layers[k]}, device_id_type=MESH,
        )

    def x_copy(k, c):
        return pltpu.make_async_remote_copy(
            src_ref=x_ref.at[:, columns(c, layers[k])], dst_ref=xz.at[k, c],
            send_sem=x_send.at[k, c], recv_sem=x_recv.at[k, c],
            device_id={"rep": layers[k]}, device_id_type=MESH,
        )

    def p_copy(k, j):
        to_e = (e_me + j // group) % EXPERTS
        to_c = (c_me + j % group) % group
        return pltpu.make_async_remote_copy(
            src_ref=ps.at[k, to_e, to_c], dst_ref=rb.at[k, me],
            send_sem=p_send.at[k, j], recv_sem=p_recv.at[k, j],
            device_id={"exp": to_e * group + to_c}, device_id_type=MESH,
        )

    def q_copy(k, j):
        to = (me + j) % q
        return pltpu.make_async_remote_copy(
            src_ref=qs.at[k, to // group, to % group], dst_ref=xb.at[k, me],
            send_sem=q_send.at[k, j], recv_sem=q_recv.at[k, j],
            device_id={"exp": to}, device_id_type=MESH,
        )

    def h_copy(k, m):
        to = e_me * group + (c_me + group - m) % group
        return pltpu.make_async_remote_copy(
            src_ref=rb.at[k], dst_ref=ph.at[m - 1, k],
            send_sem=h_send.at[k, m], recv_sem=h_recv.at[k, m],
            device_id={"exp": to}, device_id_type=MESH,
        )

    def b_copy(k, j):
        to = (me + j) % q
        return pltpu.make_async_remote_copy(
            src_ref=db.at[k, to], dst_ref=bk.at[k, c_me, e_me],
            send_sem=b_send.at[k, j], recv_sem=b_recv.at[k, j],
            device_id={"exp": to}, device_id_type=MESH,
        )

    def u_copy(k):
        return pltpu.make_async_remote_copy(
            src_ref=us.at[k], dst_ref=fin.at[k], send_sem=u_send.at[k], recv_sem=u_recv.at[k],
            device_id={"rep": layers[k]}, device_id_type=MESH,
        )

    def g_start(step, m):
        for way in range(2):
            @pl.when(g_sends(way, step))
            def _():
                g_copy(way, step, m).start()

    def g_land(step, m):
        for way in range(2):
            @pl.when(g_lands(way, step))
            def _():
                g_copy(way, step, m).wait_recv()

    def pack(k, m):
        part = jnp.dot(rz[k], gz[layers[k], :, hidden_at(m)], preferred_element_type=jnp.float32)
        ps[k, :, (c_me + m) % group] = part.astype(jnp.bfloat16).reshape(EXPERTS, CAP, half)
        for j in range(m, q, group):
            if j:
                p_copy(k, j).start()
        if m == 0:
            rb[k, me] = ps[k, e_me, c_me]

    def x_starts(step):
        for k in range(1, n):
            to = layers[k]
            @pl.when(((to > z) & (to == step)) | ((to < z) & (to == n - 1 - step)))
            def _():
                for c in range(group):
                    x_copy(k, c).start()

    def x_pack(k):
        for c in range(group):
            if k:
                x_copy(k, c).wait_recv()
            else:
                own_copy(c).wait()
            part = jnp.dot(rz[k], xz[k, c], preferred_element_type=jnp.float32)
            qs[k, :, c] = part.astype(jnp.bfloat16).reshape(EXPERTS, CAP, piece)
        for j in range(1, q):
            q_copy(k, j).start()
        xb[k, me] = qs[k, e_me, c_me]

    def x_turn(k):
        for j in range(1, q):
            q_copy(k, j).wait_recv()
        xt[:, k * rows : (k + 1) * rows] = xb[k].reshape(rows, piece).T

    def exchange(k):
        for j in range(1, q):
            p_copy(k, j).wait_recv()
        for m in range(1, group):
            h_copy(k, m).start()

    def tile_copy(m, at):
        start = pl.multiple_of((c_me + m) % group * half + at, 256)
        return pltpu.make_async_copy(
            wf.at[:, m * half + at : m * half + at + 256], wg_ref.at[:, pl.ds(start, 256)],
            tile_sem.at[(m * half + at) // 256],
        )

    def weight_rows(first, last):
        for m in range(group):
            for at in range(0, half, 256):
                total = None
                for k in range(first, last):
                    lhs = xt[:, k * rows : (k + 1) * rows]
                    if m == 0:
                        rhs = rb[k, :, :, at : at + 256]
                    else:
                        rhs = ph[m - 1, k, :, :, at : at + 256]
                    part = jnp.dot(lhs, rhs.reshape(rows, 256), preferred_element_type=jnp.float32)
                    total = part if total is None else total + part
                if first:
                    total = total + wf[:, m * half + at : m * half + at + 256]
                wf[:, m * half + at : m * half + at + 256] = total
                if last == n:
                    tile_copy(m, at).start()

    def grads_of(k, m):
        if m == 0:
            return rb[k].reshape(rows, half)
        return ph[m - 1, k].reshape(rows, half)

    def input_rows(k):
        total = None
        for m in range(group):
            if m:
                h_copy(k, m).wait_recv()
            part = lax.dot_general(
                grads_of(k, m), wb[:, hidden_at(m)], (((1,), (1,)), ((), ())),
                preferred_element_type=jnp.float32,
            )
            total = part if total is None else total + part
        db[k] = total.astype(jnp.bfloat16).reshape(q, CAP, piece)
        for j in range(1, q):
            b_copy(k, j).start()
        bk[k, c_me, e_me] = db[k, me]

    def unpack(k):
        for j in range(1, q):
            b_copy(k, j).wait_recv()
        for c in range(group):
            part = lax.dot_general(
                rz[k], bk[k, c].reshape(slots, piece), (((0,), (0,)), ((), ())),
                preferred_element_type=jnp.float32,
            )
            part = part.astype(jnp.bfloat16)
            if k:
                us[k, c] = part
            else:
                dx_ref[:, columns(c, z)] = part
        if k:
            u_copy(k).start()

    for m in range(group):
        g_start(0, m)
    for k in range(1, n):
        r_copy(k).start()
    for m in range(group):
        pack(0, m)
    x_pack(0)
    weights.wait()
    wb[...] = wf[...].astype(jnp.bfloat16)
    for k in range(1, n):
        r_copy(k).wait_recv()
        for m in range(group):
            g_land(k - 1, m)
            if k < n - 1:
                g_start(k, m)
            pack(k, m)
        x_starts(k)
        exchange(k - 1)
        if k >= 2:
            input_rows(k - 2)
        if k >= 3:
            unpack(k - 3)
    input_rows(n - 2)
    for k in range(max(n - 3, 0), n - 2):
        unpack(k)
    exchange(n - 1)
    x_pack(1)
    input_rows(n - 1)
    unpack(n - 2)
    for k in range(2, n - 1):
        x_pack(k)
    unpack(n - 1)
    if n > 2:
        x_pack(n - 1)
    for k in range(n // 2):
        x_turn(k)
    weight_rows(0, n // 2)
    for k in range(n // 2, n):
        x_turn(k)
    weight_rows(n // 2, n)
    for k in range(1, n):
        u_copy(k).wait_recv()
        for c in range(group):
            dx_ref[:, columns(c, layers[k])] = fin[k, c]
    for m in range(group):
        for at in range(0, half, 256):
            tile_copy(m, at).wait()

    for step in range(n - 1):
        for way in range(2):
            @pl.when(g_sends(way, step))
            def _():
                for m in range(group):
                    g_copy(way, step, m).wait_send()
    for k in range(n):
        if k:
            r_copy(k).wait_send()
            for c in range(group):
                x_copy(k, c).wait_send()
            u_copy(k).wait_send()
        for j in range(1, q):
            p_copy(k, j).wait_send()
            q_copy(k, j).wait_send()
            b_copy(k, j).wait_send()
        for m in range(1, group):
            h_copy(k, m).wait_send()


def tokens_move(
    activations,
    grad_hidden,
    pre_gate,
    pre_up,
    modality,
    expert_index,
    master,
    first_moment,
    second_moment,
):
    n = lax.axis_size("rep")
    q = lax.axis_size("exp")
    group = q // EXPERTS
    tok, width = activations.shape
    piece, hid2 = master.shape
    half = hid2 // group
    expert = 2 * modality + expert_index
    onehot = (expert[:, None] == jnp.arange(EXPERTS, dtype=jnp.int32)[None, :]).astype(jnp.int32)
    before = jnp.cumsum(onehot, axis=0) - onehot
    slot_pos = jnp.sum(before * onehot, axis=1)
    place = expert * CAP + slot_pos
    routing = place[None, :] == jnp.arange(EXPERTS * CAP, dtype=jnp.int32)[:, None]
    routing = routing.astype(jnp.bfloat16)
    vmem = pl.BlockSpec(memory_space=pltpu.VMEM)
    anywhere = pl.BlockSpec(memory_space=pl.ANY)
    bf16 = jnp.bfloat16
    dma = pltpu.SemaphoreType.DMA
    input_grad, weight_grad = pl.pallas_call(
        rows_kernel,
        out_shape=(
            jax.ShapeDtypeStruct((tok, width), bf16),
            jax.ShapeDtypeStruct((piece, hid2), jnp.float32),
        ),
        in_specs=[anywhere, vmem, vmem, vmem, vmem, anywhere],
        out_specs=(vmem, anywhere),
        scratch_shapes=[
            pltpu.VMEM((n, tok, hid2), bf16),
            pltpu.VMEM((n, group, tok, piece), bf16),
            pltpu.VMEM((n, EXPERTS * CAP, tok), bf16),
            pltpu.VMEM((n, EXPERTS, group, CAP, half), bf16),
            pltpu.VMEM((n, q, CAP, half), bf16),
            pltpu.VMEM((n, EXPERTS, group, CAP, piece), bf16),
            pltpu.VMEM((n, q, CAP, piece), bf16),
            pltpu.VMEM((group - 1, n, q, CAP, half), bf16),
            pltpu.VMEM((piece, hid2), jnp.float32),
            pltpu.VMEM((piece, hid2), bf16),
            pltpu.VMEM((piece, n * q * CAP), bf16),
            pltpu.VMEM((n, q, CAP, piece), bf16),
            pltpu.VMEM((n, group, EXPERTS, CAP, piece), bf16),
            pltpu.VMEM((n, group, tok, piece), bf16),
            pltpu.VMEM((n, group, tok, piece), bf16),
            dma((2, n, group)), dma((2, n, group)),
            dma((n, group)), dma((n, group)),
            dma((n,)), dma((n,)),
            dma((n, q)), dma((n, q)),
            dma((n, q)), dma((n, q)),
            dma((n, group)), dma((n, group)),
            dma((n, q)), dma((n, q)),
            dma((n,)), dma((n,)),
            dma((group,)), dma((hid2 // 256,)),
            dma,
        ],
        compiler_params=pltpu.CompilerParams(
            collective_id=0, has_side_effects=True, vmem_limit_bytes=VMEM_GRANT
        ),
        name="rows_kernel",
    )(activations, grad_hidden, pre_gate, pre_up, routing, master)
    new_first = beta_one * first_moment + (1.0 - beta_one) * weight_grad
    new_second = beta_two * second_moment + (1.0 - beta_two) * weight_grad * weight_grad
    corr_one = 1.0 - beta_one**adam_count
    corr_two = 1.0 - beta_two**adam_count
    update = new_first / corr_one / (jnp.sqrt(new_second / corr_two) + adam_eps)
    new_master = master - learn_rate * update
    return (input_grad, new_master, new_first, new_second)


def body(*blocks):
    n = lax.axis_size("rep")
    q = lax.axis_size("exp")
    group = q // EXPERTS
    tok, width = blocks[0].shape
    piece, hid2 = blocks[6].shape
    held = n * q * CAP * (hid2 + 4 * piece) * 2 + 12 * piece * hid2
    held += n * tok * (hid2 + 3 * group * piece) * 2 + n * EXPERTS * CAP * group * hid2
    fits = held <= VMEM_GRANT and group >= 2 and n >= 2 and n & (n - 1) == 0
    if fits and piece % 128 == 0 and hid2 % 512 == 0 and hid2 // group % 256 == 0 and q * CAP % 128 == 0:
        return tokens_move(*blocks)
    return weights_move(*blocks)


def solution(mesh):
    in_specs = (
        P(("rep", "exp"), None),
        P(("rep", "exp"), None),
        P(("rep", "exp"), None),
        P(("rep", "exp"), None),
        P(("rep", "exp")),
        P(("rep", "exp")),
        P(("exp", "rep"), None),
        P(("exp", "rep"), None),
        P(("exp", "rep"), None),
    )
    out_specs = (
        P(("rep", "exp"), None),
        P(("exp", "rep"), None),
        P(("exp", "rep"), None),
        P(("exp", "rep"), None),
    )
    return jax.shard_map(body, mesh=mesh, in_specs=in_specs, out_specs=out_specs, check_vma=False)
```

```python
import jax
import jax.numpy as jnp
from jax import lax
from jax.experimental import pallas as pl
from jax.experimental.pallas import tpu as pltpu
from jax.sharding import PartitionSpec as P

EXPERTS = 4
CAP = 48


beta_one = 0.9
beta_two = 0.999
learn_rate = 0.02
adam_eps = 1e-08
adam_count = 1000


def from_partner(block, axis, stride):
    count = lax.axis_size(axis)
    route = []
    for low in range(count):
        high = low | 1 << stride
        if high != low and high < count:
            route += [(low, high), (high, low)]
    return lax.ppermute(block, axis, route)


def hidden_grads(saved_rows):
    grad_val = saved_rows[:, 0].astype(jnp.float32)
    gate_val = saved_rows[:, 1].astype(jnp.float32)
    up_val = saved_rows[:, 2].astype(jnp.float32)
    sig = 1.0 / (1.0 + jnp.exp(-gate_val))
    grad_gate = (grad_val * up_val * sig * (1.0 + gate_val * (1.0 - sig))).astype(jnp.bfloat16)
    grad_up = (grad_val * gate_val * sig).astype(jnp.bfloat16)
    return jnp.stack([grad_gate, grad_up], axis=1)


def weights_move(
    activations,
    grad_hidden,
    pre_gate,
    pre_up,
    modality,
    expert_index,
    master,
    first_moment,
    second_moment,
):
    tok_count = activations.shape[0]
    width = activations.shape[1]
    hidden = grad_hidden.shape[1]
    exp_size = lax.axis_size("exp")
    group = exp_size // EXPERTS
    piece_width = width // group
    piece_hidden = hidden // group
    capacity = CAP
    rows_total = exp_size * capacity
    expert = 2 * modality + expert_index
    onehot = (expert[:, None] == jnp.arange(EXPERTS, dtype=jnp.int32)[None, :]).astype(jnp.int32)
    before = jnp.cumsum(onehot, axis=0) - onehot
    slot_pos = jnp.sum(before * onehot, axis=1)
    same_expert = expert[None, None, :] == jnp.arange(EXPERTS, dtype=jnp.int32)[:, None, None]
    same_slot = slot_pos[None, None, :] == jnp.arange(capacity, dtype=jnp.int32)[None, :, None]
    routing = (same_expert & same_slot).astype(jnp.bfloat16)
    x_split = activations.reshape(tok_count, group, piece_width)
    x_send = jnp.einsum("ect,tgd->egcd", routing, x_split, preferred_element_type=jnp.float32)
    x_send = x_send.astype(jnp.bfloat16).reshape(EXPERTS * group, capacity, piece_width)
    saved = jnp.stack([grad_hidden, pre_gate, pre_up], axis=1)
    split_saved = saved.reshape(tok_count, 3, group, piece_hidden)
    parts = jnp.einsum("ect,tsgh->egcsh", routing, split_saved, preferred_element_type=jnp.float32)
    parts = parts.astype(jnp.bfloat16).reshape(EXPERTS * group, capacity, 3 * piece_hidden)
    x_recv, h_recv = (
        lax.all_to_all(x_send, "exp", split_axis=0, concat_axis=0, tiled=True),
        lax.all_to_all(parts, "exp", split_axis=0, concat_axis=0, tiled=True),
    )
    local = hidden_grads(h_recv.reshape(rows_total, 3, piece_hidden))
    blocks = local[None]
    position = lax.axis_index("exp")
    for level in range(group.bit_length() - 1):
        partner = from_partner(blocks, "exp", level)
        upper = position // 2**level % 2 == 1
        blocks = jnp.where(
            upper,
            jnp.concatenate([partner, blocks], axis=0),
            jnp.concatenate([blocks, partner], axis=0),
        )
    grads_flat = jnp.transpose(blocks, (1, 2, 0, 3)).reshape(rows_total, 2 * hidden)
    x_rows = x_recv.reshape(rows_total, piece_width)
    shard_bf = master.astype(jnp.bfloat16)
    dx_rows = lax.dot_general(
        grads_flat,
        lax.all_gather(shard_bf, "rep", axis=0, tiled=True),
        (((1,), (1,)), ((), ())),
        preferred_element_type=jnp.float32,
    )
    dx_send = dx_rows.astype(jnp.bfloat16).reshape(exp_size, capacity, piece_width)
    back = lax.all_to_all(dx_send, "exp", split_axis=0, concat_axis=0, tiled=True)
    back = back.reshape(EXPERTS, group, capacity, piece_width)
    input_grad = jnp.einsum("ect,egcd->tgd", routing, back, preferred_element_type=jnp.float32)
    input_grad = input_grad.reshape(tok_count, width).astype(jnp.bfloat16)
    weight_grad = lax.psum_scatter(
        lax.dot_general(
            x_rows, grads_flat, (((0,), (0,)), ((), ())), preferred_element_type=jnp.float32
        ).astype(jnp.bfloat16),
        "rep",
        scatter_dimension=0,
        tiled=True,
    ).astype(jnp.float32)
    new_first = beta_one * first_moment + (1.0 - beta_one) * weight_grad
    new_second = beta_two * second_moment + (1.0 - beta_two) * weight_grad * weight_grad
    corr_one = 1.0 - beta_one**adam_count
    corr_two = 1.0 - beta_two**adam_count
    update = new_first / corr_one / (jnp.sqrt(new_second / corr_two) + adam_eps)
    new_master = master - learn_rate * update
    return (input_grad, new_master, new_first, new_second)


MESH = pl.DeviceIdType.MESH
VMEM_GRANT = 56 * 2**20


def flip(position, mask, count):
    out = 0
    bit = 1
    while bit < count:
        have = position // bit % 2
        out = out + bit * ((1 - have) if mask & bit else have)
        bit *= 2
    return out


def rows_kernel(
    x_ref, grad_ref, gate_ref, up_ref, mode_ref, index_ref, master_ref,
    dx_ref, wg_ref,
    gz, xz, rz, ps, rb, qs, xb, ph, wf, wb, xt, db, bk, us, fin,
    g_send, g_recv, x_send, x_recv, r_send, r_recv,
    p_send, p_recv, q_send, q_recv, h_send, h_recv,
    b_send, b_recv, u_send, u_recv, own_sem, tile_sem, w_sem,
):
    n = lax.axis_size("rep")
    q = lax.axis_size("exp")
    z = lax.axis_index("rep")
    me = lax.axis_index("exp")
    group = q // EXPERTS
    e_me = me // group
    c_me = me % group
    tok = x_ref.shape[0]
    width = x_ref.shape[1]
    piece = master_ref.shape[0]
    hid2 = master_ref.shape[1]
    half = hid2 // group
    strip = width // group
    slots = EXPERTS * CAP
    rows = q * CAP
    layers = [flip(z, k, n) for k in range(n)]

    def columns(c, layer):
        return pl.ds(pl.multiple_of(c * strip + layer * piece, piece), piece)

    def own_copy(c):
        return pltpu.make_async_copy(x_ref.at[:, columns(c, z)], xz.at[0, c], own_sem.at[c])

    weights = pltpu.make_async_copy(master_ref, wf, w_sem)
    weights.start()

    barrier = pltpu.get_barrier_semaphore()
    for k in range(1, n):
        pl.semaphore_signal(barrier, inc=1, device_id={"rep": layers[k]}, device_id_type=MESH)
    for j in range(1, q):
        pl.semaphore_signal(barrier, inc=1, device_id={"exp": (me + j) % q}, device_id_type=MESH)
    for c in range(group):
        own_copy(c).start()
    hidden = grad_ref.shape[1]
    for at in range(0, hidden, 256):
        grad_val = grad_ref[:, at : at + 256].astype(jnp.float32)
        gate_val = gate_ref[:, at : at + 256].astype(jnp.float32)
        up_val = up_ref[:, at : at + 256].astype(jnp.float32)
        sig = 1.0 / (1.0 + jnp.exp(-gate_val))
        grad_gate = grad_val * up_val * sig * (1.0 + gate_val * (1.0 - sig))
        gz[z, :, at : at + 256] = grad_gate.astype(jnp.bfloat16)
        grad_up = grad_val * gate_val * sig
        gz[z, :, hidden + at : hidden + at + 256] = grad_up.astype(jnp.bfloat16)
    expert = 2 * mode_ref[...] + index_ref[...]
    lanes = lax.broadcasted_iota(jnp.int32, (tok, tok), 1)
    earlier = lax.broadcasted_iota(jnp.int32, (tok, tok), 0) < lanes
    onehot = lax.broadcasted_iota(jnp.int32, (16, tok), 0) == expert
    onehot = onehot.astype(jnp.float32)
    before = jnp.dot(
        onehot.astype(jnp.bfloat16), earlier.astype(jnp.float32).astype(jnp.bfloat16),
        preferred_element_type=jnp.float32,
    )
    place = expert.astype(jnp.float32) * CAP + jnp.sum(before * onehot, axis=0, keepdims=True)
    slot = lax.broadcasted_iota(jnp.int32, (slots, tok), 0).astype(jnp.float32)
    rz[0] = (slot == place).astype(jnp.float32).astype(jnp.bfloat16)
    pl.semaphore_wait(barrier, n + q - 2)

    def hidden_at(m):
        return pl.ds(pl.multiple_of((c_me + m) % group * half, half), half)

    def g_copy(way, step, m):
        block = z - step if way == 0 else z + step
        to = z + 1 if way == 0 else z - 1
        return pltpu.make_async_remote_copy(
            src_ref=gz.at[block, :, hidden_at(m)], dst_ref=gz.at[block, :, hidden_at(m)],
            send_sem=g_send.at[way, step, m], recv_sem=g_recv.at[way, step, m],
            device_id={"rep": to}, device_id_type=MESH,
        )

    def g_sends(way, step):
        return (z >= step) & (z < n - 1) if way == 0 else (z + step < n) & (z > 0)

    def g_lands(way, step):
        return z - 1 - step >= 0 if way == 0 else z + 1 + step < n

    def r_copy(k):
        return pltpu.make_async_remote_copy(
            src_ref=rz.at[0], dst_ref=rz.at[k], send_sem=r_send.at[k], recv_sem=r_recv.at[k],
            device_id={"rep": layers[k]}, device_id_type=MESH,
        )

    def x_copy(k, c):
        return pltpu.make_async_remote_copy(
            src_ref=x_ref.at[:, columns(c, layers[k])], dst_ref=xz.at[k, c],
            send_sem=x_send.at[k, c], recv_sem=x_recv.at[k, c],
            device_id={"rep": layers[k]}, device_id_type=MESH,
        )

    def p_copy(k, j):
        to_e = (e_me + j // group) % EXPERTS
        to_c = (c_me + j % group) % group
        return pltpu.make_async_remote_copy(
            src_ref=ps.at[k, to_e, to_c], dst_ref=rb.at[k, me],
            send_sem=p_send.at[k, j], recv_sem=p_recv.at[k, j],
            device_id={"exp": to_e * group + to_c}, device_id_type=MESH,
        )

    def q_copy(k, j):
        to = (me + j) % q
        return pltpu.make_async_remote_copy(
            src_ref=qs.at[k, to // group, to % group], dst_ref=xb.at[k, me],
            send_sem=q_send.at[k, j], recv_sem=q_recv.at[k, j],
            device_id={"exp": to}, device_id_type=MESH,
        )

    def h_copy(k, m):
        to = e_me * group + (c_me + group - m) % group
        return pltpu.make_async_remote_copy(
            src_ref=rb.at[k], dst_ref=ph.at[m - 1, k],
            send_sem=h_send.at[k, m], recv_sem=h_recv.at[k, m],
            device_id={"exp": to}, device_id_type=MESH,
        )

    def b_copy(k, j):
        to = (me + j) % q
        return pltpu.make_async_remote_copy(
            src_ref=db.at[k, to], dst_ref=bk.at[k, c_me, e_me],
            send_sem=b_send.at[k, j], recv_sem=b_recv.at[k, j],
            device_id={"exp": to}, device_id_type=MESH,
        )

    def u_copy(k):
        return pltpu.make_async_remote_copy(
            src_ref=us.at[k], dst_ref=fin.at[k], send_sem=u_send.at[k], recv_sem=u_recv.at[k],
            device_id={"rep": layers[k]}, device_id_type=MESH,
        )

    def g_start(step, m):
        for way in range(2):
            @pl.when(g_sends(way, step))
            def _():
                g_copy(way, step, m).start()

    def g_land(step, m):
        for way in range(2):
            @pl.when(g_lands(way, step))
            def _():
                g_copy(way, step, m).wait_recv()

    def pack(k, m):
        part = jnp.dot(rz[k], gz[layers[k], :, hidden_at(m)], preferred_element_type=jnp.float32)
        ps[k, :, (c_me + m) % group] = part.astype(jnp.bfloat16).reshape(EXPERTS, CAP, half)
        for j in range(m, q, group):
            if j:
                p_copy(k, j).start()
        if m == 0:
            rb[k, me] = ps[k, e_me, c_me]

    at_end = (z == 0) | (z == n - 1)

    def x_starts(step, who=None):
        for k in range(1, n):
            to = layers[k]
            free = ((to > z) & (to == step)) | ((to < z) & (to == n - 1 - step))
            @pl.when(free if who is None else free & who)
            def _():
                for c in range(group):
                    x_copy(k, c).start()

    def x_pack(k):
        for c in range(group):
            if k:
                x_copy(k, c).wait_recv()
            else:
                own_copy(c).wait()
            part = jnp.dot(rz[k], xz[k, c], preferred_element_type=jnp.float32)
            qs[k, :, c] = part.astype(jnp.bfloat16).reshape(EXPERTS, CAP, piece)
        for j in range(1, q):
            q_copy(k, j).start()
        xb[k, me] = qs[k, e_me, c_me]

    def x_turn(k):
        for j in range(1, q):
            q_copy(k, j).wait_recv()
        xt[:, k * rows : (k + 1) * rows] = xb[k].reshape(rows, piece).T

    def exchange(k):
        for j in range(1, q):
            p_copy(k, j).wait_recv()
        for m in range(1, group):
            h_copy(k, m).start()

    def tile_copy(m, at):
        start = pl.multiple_of((c_me + m) % group * half + at, 256)
        return pltpu.make_async_copy(
            wf.at[:, m * half + at : m * half + at + 256], wg_ref.at[:, pl.ds(start, 256)],
            tile_sem.at[(m * half + at) // 256],
        )

    def weight_rows(first, last):
        for m in range(group):
            for at in range(0, half, 256):
                total = None
                for k in range(first, last):
                    lhs = xt[:, k * rows : (k + 1) * rows]
                    if m == 0:
                        rhs = rb[k, :, :, at : at + 256]
                    else:
                        rhs = ph[m - 1, k, :, :, at : at + 256]
                    part = jnp.dot(lhs, rhs.reshape(rows, 256), preferred_element_type=jnp.float32)
                    total = part if total is None else total + part
                if first:
                    total = total + wf[:, m * half + at : m * half + at + 256]
                wf[:, m * half + at : m * half + at + 256] = total
                if last == n:
                    tile_copy(m, at).start()

    def grads_of(k, m):
        if m == 0:
            return rb[k].reshape(rows, half)
        return ph[m - 1, k].reshape(rows, half)

    def input_rows(k):
        total = None
        for m in range(group):
            if m:
                h_copy(k, m).wait_recv()
            part = lax.dot_general(
                grads_of(k, m), wb[:, hidden_at(m)], (((1,), (1,)), ((), ())),
                preferred_element_type=jnp.float32,
            )
            total = part if total is None else total + part
        db[k] = total.astype(jnp.bfloat16).reshape(q, CAP, piece)
        for j in range(1, q):
            b_copy(k, j).start()
        bk[k, c_me, e_me] = db[k, me]

    def unpack(k):
        for j in range(1, q):
            b_copy(k, j).wait_recv()
        for c in range(group):
            part = lax.dot_general(
                rz[k], bk[k, c].reshape(slots, piece), (((0,), (0,)), ((), ())),
                preferred_element_type=jnp.float32,
            )
            part = part.astype(jnp.bfloat16)
            if k:
                us[k, c] = part
            else:
                dx_ref[:, columns(c, z)] = part
        if k:
            u_copy(k).start()

    for m in range(group):
        g_start(0, m)
    for k in range(1, n):
        r_copy(k).start()
    for m in range(group):
        pack(0, m)
    x_pack(0)
    weights.wait()
    wb[...] = wf[...].astype(jnp.bfloat16)
    for k in range(1, n):
        r_copy(k).wait_recv()
        for m in range(group):
            g_land(k - 1, m)
            if k < n - 1:
                g_start(k, m)
            pack(k, m)
        x_starts(k, at_end if k == n - 1 else None)
        exchange(k - 1)
        if k >= 2:
            input_rows(k - 2)
        if k >= 3:
            unpack(k - 3)
    input_rows(n - 2)
    for k in range(max(n - 3, 0), n - 2):
        unpack(k)
    exchange(n - 1)
    x_starts(n - 1, jnp.logical_not(at_end))
    x_pack(1)
    input_rows(n - 1)
    unpack(n - 2)
    for k in range(2, n - 1):
        x_pack(k)
    unpack(n - 1)
    if n > 2:
        x_pack(n - 1)
    for k in range(n // 2):
        x_turn(k)
    weight_rows(0, n // 2)
    for k in range(n // 2, n):
        x_turn(k)
    weight_rows(n // 2, n)
    for k in range(1, n):
        u_copy(k).wait_recv()
        for c in range(group):
            dx_ref[:, columns(c, layers[k])] = fin[k, c]
    for m in range(group):
        for at in range(0, half, 256):
            tile_copy(m, at).wait()

    for step in range(n - 1):
        for way in range(2):
            @pl.when(g_sends(way, step))
            def _():
                for m in range(group):
                    g_copy(way, step, m).wait_send()
    for k in range(n):
        if k:
            r_copy(k).wait_send()
            for c in range(group):
                x_copy(k, c).wait_send()
            u_copy(k).wait_send()
        for j in range(1, q):
            p_copy(k, j).wait_send()
            q_copy(k, j).wait_send()
            b_copy(k, j).wait_send()
        for m in range(1, group):
            h_copy(k, m).wait_send()


def tokens_move(
    activations,
    grad_hidden,
    pre_gate,
    pre_up,
    modality,
    expert_index,
    master,
    first_moment,
    second_moment,
):
    n = lax.axis_size("rep")
    q = lax.axis_size("exp")
    group = q // EXPERTS
    tok, width = activations.shape
    piece, hid2 = master.shape
    half = hid2 // group
    vmem = pl.BlockSpec(memory_space=pltpu.VMEM)
    anywhere = pl.BlockSpec(memory_space=pl.ANY)
    bf16 = jnp.bfloat16
    dma = pltpu.SemaphoreType.DMA
    input_grad, weight_grad = pl.pallas_call(
        rows_kernel,
        out_shape=(
            jax.ShapeDtypeStruct((tok, width), bf16),
            jax.ShapeDtypeStruct((piece, hid2), jnp.float32),
        ),
        in_specs=[anywhere, vmem, vmem, vmem, vmem, vmem, anywhere],
        out_specs=(vmem, anywhere),
        scratch_shapes=[
            pltpu.VMEM((n, tok, hid2), bf16),
            pltpu.VMEM((n, group, tok, piece), bf16),
            pltpu.VMEM((n, EXPERTS * CAP, tok), bf16),
            pltpu.VMEM((n, EXPERTS, group, CAP, half), bf16),
            pltpu.VMEM((n, q, CAP, half), bf16),
            pltpu.VMEM((n, EXPERTS, group, CAP, piece), bf16),
            pltpu.VMEM((n, q, CAP, piece), bf16),
            pltpu.VMEM((group - 1, n, q, CAP, half), bf16),
            pltpu.VMEM((piece, hid2), jnp.float32),
            pltpu.VMEM((piece, hid2), bf16),
            pltpu.VMEM((piece, n * q * CAP), bf16),
            pltpu.VMEM((n, q, CAP, piece), bf16),
            pltpu.VMEM((n, group, EXPERTS, CAP, piece), bf16),
            pltpu.VMEM((n, group, tok, piece), bf16),
            pltpu.VMEM((n, group, tok, piece), bf16),
            dma((2, n, group)), dma((2, n, group)),
            dma((n, group)), dma((n, group)),
            dma((n,)), dma((n,)),
            dma((n, q)), dma((n, q)),
            dma((n, q)), dma((n, q)),
            dma((n, group)), dma((n, group)),
            dma((n, q)), dma((n, q)),
            dma((n,)), dma((n,)),
            dma((group,)), dma((hid2 // 256,)),
            dma,
        ],
        compiler_params=pltpu.CompilerParams(
            collective_id=0, has_side_effects=True, vmem_limit_bytes=VMEM_GRANT
        ),
        name="rows_kernel",
    )(
        activations, grad_hidden, pre_gate, pre_up,
        modality.reshape(1, tok), expert_index.reshape(1, tok), master,
    )
    new_first = beta_one * first_moment + (1.0 - beta_one) * weight_grad
    new_second = beta_two * second_moment + (1.0 - beta_two) * weight_grad * weight_grad
    corr_one = 1.0 - beta_one**adam_count
    corr_two = 1.0 - beta_two**adam_count
    update = new_first / corr_one / (jnp.sqrt(new_second / corr_two) + adam_eps)
    new_master = master - learn_rate * update
    return (input_grad, new_master, new_first, new_second)


def body(*blocks):
    n = lax.axis_size("rep")
    q = lax.axis_size("exp")
    group = q // EXPERTS
    tok, width = blocks[0].shape
    piece, hid2 = blocks[6].shape
    held = n * q * CAP * (hid2 + 4 * piece) * 2 + 12 * piece * hid2
    held += n * tok * (hid2 + 3 * group * piece) * 2 + n * EXPERTS * CAP * group * hid2
    fits = held <= VMEM_GRANT * 3 // 4 and group >= 2 and n >= 2 and n & (n - 1) == 0
    if fits and piece % 128 == 0 and hid2 % 512 == 0 and hid2 // group % 256 == 0 and q * CAP % 128 == 0:
        return tokens_move(*blocks)
    return weights_move(*blocks)


def solution(mesh):
    in_specs = (
        P(("rep", "exp"), None),
        P(("rep", "exp"), None),
        P(("rep", "exp"), None),
        P(("rep", "exp"), None),
        P(("rep", "exp")),
        P(("rep", "exp")),
        P(("exp", "rep"), None),
        P(("exp", "rep"), None),
        P(("exp", "rep"), None),
    )
    out_specs = (
        P(("rep", "exp"), None),
        P(("exp", "rep"), None),
        P(("exp", "rep"), None),
        P(("exp", "rep"), None),
    )
    return jax.shard_map(body, mesh=mesh, in_specs=in_specs, out_specs=out_specs, check_vma=False)
```

```python
import jax
import jax.numpy as jnp
from jax import lax
from jax.experimental import pallas as pl
from jax.experimental.pallas import tpu as pltpu
from jax.sharding import PartitionSpec as P

EXPERTS = 4
CAP = 48


beta_one = 0.9
beta_two = 0.999
learn_rate = 0.02
adam_eps = 1e-08
adam_count = 1000


def from_partner(block, axis, stride):
    count = lax.axis_size(axis)
    route = []
    for low in range(count):
        high = low | 1 << stride
        if high != low and high < count:
            route += [(low, high), (high, low)]
    return lax.ppermute(block, axis, route)


def hidden_grads(saved_rows):
    grad_val = saved_rows[:, 0].astype(jnp.float32)
    gate_val = saved_rows[:, 1].astype(jnp.float32)
    up_val = saved_rows[:, 2].astype(jnp.float32)
    sig = 1.0 / (1.0 + jnp.exp(-gate_val))
    grad_gate = (grad_val * up_val * sig * (1.0 + gate_val * (1.0 - sig))).astype(jnp.bfloat16)
    grad_up = (grad_val * gate_val * sig).astype(jnp.bfloat16)
    return jnp.stack([grad_gate, grad_up], axis=1)


def weights_move(
    activations,
    grad_hidden,
    pre_gate,
    pre_up,
    modality,
    expert_index,
    master,
    first_moment,
    second_moment,
):
    tok_count = activations.shape[0]
    width = activations.shape[1]
    hidden = grad_hidden.shape[1]
    exp_size = lax.axis_size("exp")
    group = exp_size // EXPERTS
    piece_width = width // group
    piece_hidden = hidden // group
    capacity = CAP
    rows_total = exp_size * capacity
    expert = 2 * modality + expert_index
    onehot = (expert[:, None] == jnp.arange(EXPERTS, dtype=jnp.int32)[None, :]).astype(jnp.int32)
    before = jnp.cumsum(onehot, axis=0) - onehot
    slot_pos = jnp.sum(before * onehot, axis=1)
    same_expert = expert[None, None, :] == jnp.arange(EXPERTS, dtype=jnp.int32)[:, None, None]
    same_slot = slot_pos[None, None, :] == jnp.arange(capacity, dtype=jnp.int32)[None, :, None]
    routing = (same_expert & same_slot).astype(jnp.bfloat16)
    x_split = activations.reshape(tok_count, group, piece_width)
    x_send = jnp.einsum("ect,tgd->egcd", routing, x_split, preferred_element_type=jnp.float32)
    x_send = x_send.astype(jnp.bfloat16).reshape(EXPERTS * group, capacity, piece_width)
    saved = jnp.stack([grad_hidden, pre_gate, pre_up], axis=1)
    split_saved = saved.reshape(tok_count, 3, group, piece_hidden)
    parts = jnp.einsum("ect,tsgh->egcsh", routing, split_saved, preferred_element_type=jnp.float32)
    parts = parts.astype(jnp.bfloat16).reshape(EXPERTS * group, capacity, 3 * piece_hidden)
    x_recv, h_recv = (
        lax.all_to_all(x_send, "exp", split_axis=0, concat_axis=0, tiled=True),
        lax.all_to_all(parts, "exp", split_axis=0, concat_axis=0, tiled=True),
    )
    local = hidden_grads(h_recv.reshape(rows_total, 3, piece_hidden))
    blocks = local[None]
    position = lax.axis_index("exp")
    for level in range(group.bit_length() - 1):
        partner = from_partner(blocks, "exp", level)
        upper = position // 2**level % 2 == 1
        blocks = jnp.where(
            upper,
            jnp.concatenate([partner, blocks], axis=0),
            jnp.concatenate([blocks, partner], axis=0),
        )
    grads_flat = jnp.transpose(blocks, (1, 2, 0, 3)).reshape(rows_total, 2 * hidden)
    x_rows = x_recv.reshape(rows_total, piece_width)
    shard_bf = master.astype(jnp.bfloat16)
    dx_rows = lax.dot_general(
        grads_flat,
        lax.all_gather(shard_bf, "rep", axis=0, tiled=True),
        (((1,), (1,)), ((), ())),
        preferred_element_type=jnp.float32,
    )
    dx_send = dx_rows.astype(jnp.bfloat16).reshape(exp_size, capacity, piece_width)
    back = lax.all_to_all(dx_send, "exp", split_axis=0, concat_axis=0, tiled=True)
    back = back.reshape(EXPERTS, group, capacity, piece_width)
    input_grad = jnp.einsum("ect,egcd->tgd", routing, back, preferred_element_type=jnp.float32)
    input_grad = input_grad.reshape(tok_count, width).astype(jnp.bfloat16)
    weight_grad = lax.psum_scatter(
        lax.dot_general(
            x_rows, grads_flat, (((0,), (0,)), ((), ())), preferred_element_type=jnp.float32
        ).astype(jnp.bfloat16),
        "rep",
        scatter_dimension=0,
        tiled=True,
    ).astype(jnp.float32)
    new_first = beta_one * first_moment + (1.0 - beta_one) * weight_grad
    new_second = beta_two * second_moment + (1.0 - beta_two) * weight_grad * weight_grad
    corr_one = 1.0 - beta_one**adam_count
    corr_two = 1.0 - beta_two**adam_count
    update = new_first / corr_one / (jnp.sqrt(new_second / corr_two) + adam_eps)
    new_master = master - learn_rate * update
    return (input_grad, new_master, new_first, new_second)


MESH = pl.DeviceIdType.MESH
VMEM_GRANT = 56 * 2**20


def flip(position, mask, count):
    out = 0
    bit = 1
    while bit < count:
        have = position // bit % 2
        out = out + bit * ((1 - have) if mask & bit else have)
        bit *= 2
    return out


def rows_kernel(
    x_ref, grad_ref, gate_ref, up_ref, mode_ref, index_ref, master_ref,
    dx_ref, wg_ref,
    gz, xz, rz, ps, rb, qs, xb, ph, wf, wb, xt, db, bk, us, fin,
    g_send, g_recv, x_send, x_recv, r_send, r_recv,
    p_send, p_recv, q_send, q_recv, h_send, h_recv,
    b_send, b_recv, u_send, u_recv, own_sem, tile_sem, w_sem,
):
    n = lax.axis_size("rep")
    q = lax.axis_size("exp")
    z = lax.axis_index("rep")
    me = lax.axis_index("exp")
    group = q // EXPERTS
    e_me = me // group
    c_me = me % group
    tok = x_ref.shape[0]
    width = x_ref.shape[1]
    piece = master_ref.shape[0]
    hid2 = master_ref.shape[1]
    half = hid2 // group
    strip = width // group
    slots = EXPERTS * CAP
    rows = q * CAP
    layers = [flip(z, k, n) for k in range(n)]

    def columns(c, layer):
        return pl.ds(pl.multiple_of(c * strip + layer * piece, piece), piece)

    def own_copy(c):
        return pltpu.make_async_copy(x_ref.at[:, columns(c, z)], xz.at[0, c], own_sem.at[c])

    weights = pltpu.make_async_copy(master_ref, wf, w_sem)
    weights.start()

    barrier = pltpu.get_barrier_semaphore()
    for k in range(1, n):
        pl.semaphore_signal(barrier, inc=1, device_id={"rep": layers[k]}, device_id_type=MESH)
    for j in range(1, q):
        pl.semaphore_signal(barrier, inc=1, device_id={"exp": (me + j) % q}, device_id_type=MESH)
    for c in range(group):
        own_copy(c).start()
    hidden = grad_ref.shape[1]
    for at in range(0, hidden, 256):
        grad_val = grad_ref[:, at : at + 256].astype(jnp.float32)
        gate_val = gate_ref[:, at : at + 256].astype(jnp.float32)
        up_val = up_ref[:, at : at + 256].astype(jnp.float32)
        sig = 1.0 / (1.0 + jnp.exp(-gate_val))
        grad_gate = grad_val * up_val * sig * (1.0 + gate_val * (1.0 - sig))
        gz[z, :, at : at + 256] = grad_gate.astype(jnp.bfloat16)
        grad_up = grad_val * gate_val * sig
        gz[z, :, hidden + at : hidden + at + 256] = grad_up.astype(jnp.bfloat16)
    expert = 2 * mode_ref[...] + index_ref[...]
    lanes = lax.broadcasted_iota(jnp.int32, (tok, tok), 1)
    earlier = lax.broadcasted_iota(jnp.int32, (tok, tok), 0) < lanes
    onehot = lax.broadcasted_iota(jnp.int32, (16, tok), 0) == expert
    onehot = onehot.astype(jnp.float32)
    before = jnp.dot(
        onehot.astype(jnp.bfloat16), earlier.astype(jnp.float32).astype(jnp.bfloat16),
        preferred_element_type=jnp.float32,
    )
    place = expert.astype(jnp.float32) * CAP + jnp.sum(before * onehot, axis=0, keepdims=True)
    slot = lax.broadcasted_iota(jnp.int32, (slots, tok), 0).astype(jnp.float32)
    rz[0] = (slot == place).astype(jnp.float32).astype(jnp.bfloat16)
    pl.semaphore_wait(barrier, n + q - 2)

    def hidden_at(m):
        return pl.ds(pl.multiple_of((c_me + m) % group * half, half), half)

    def g_copy(way, step, m):
        block = z - step if way == 0 else z + step
        to = z + 1 if way == 0 else z - 1
        return pltpu.make_async_remote_copy(
            src_ref=gz.at[block, :, hidden_at(m)], dst_ref=gz.at[block, :, hidden_at(m)],
            send_sem=g_send.at[way, step, m], recv_sem=g_recv.at[way, step, m],
            device_id={"rep": to}, device_id_type=MESH,
        )

    def g_sends(way, step):
        return (z >= step) & (z < n - 1) if way == 0 else (z + step < n) & (z > 0)

    def g_lands(way, step):
        return z - 1 - step >= 0 if way == 0 else z + 1 + step < n

    def r_copy(k):
        return pltpu.make_async_remote_copy(
            src_ref=rz.at[0], dst_ref=rz.at[k], send_sem=r_send.at[k], recv_sem=r_recv.at[k],
            device_id={"rep": layers[k]}, device_id_type=MESH,
        )

    def x_copy(k, c):
        return pltpu.make_async_remote_copy(
            src_ref=x_ref.at[:, columns(c, layers[k])], dst_ref=xz.at[k, c],
            send_sem=x_send.at[k, c], recv_sem=x_recv.at[k, c],
            device_id={"rep": layers[k]}, device_id_type=MESH,
        )

    def p_copy(k, j):
        to_e = (e_me + j // group) % EXPERTS
        to_c = (c_me + j % group) % group
        return pltpu.make_async_remote_copy(
            src_ref=ps.at[k, to_e, to_c], dst_ref=rb.at[k, me],
            send_sem=p_send.at[k, j], recv_sem=p_recv.at[k, j],
            device_id={"exp": to_e * group + to_c}, device_id_type=MESH,
        )

    def q_copy(k, j):
        to = (me + j) % q
        return pltpu.make_async_remote_copy(
            src_ref=qs.at[k, to // group, to % group], dst_ref=xb.at[k, me],
            send_sem=q_send.at[k, j], recv_sem=q_recv.at[k, j],
            device_id={"exp": to}, device_id_type=MESH,
        )

    def h_copy(k, m):
        to = e_me * group + (c_me + group - m) % group
        return pltpu.make_async_remote_copy(
            src_ref=rb.at[k], dst_ref=ph.at[m - 1, k],
            send_sem=h_send.at[k, m], recv_sem=h_recv.at[k, m],
            device_id={"exp": to}, device_id_type=MESH,
        )

    def b_copy(k, j):
        to = (me + j) % q
        return pltpu.make_async_remote_copy(
            src_ref=db.at[k, to], dst_ref=bk.at[k, c_me, e_me],
            send_sem=b_send.at[k, j], recv_sem=b_recv.at[k, j],
            device_id={"exp": to}, device_id_type=MESH,
        )

    def u_copy(k):
        return pltpu.make_async_remote_copy(
            src_ref=us.at[k], dst_ref=fin.at[k], send_sem=u_send.at[k], recv_sem=u_recv.at[k],
            device_id={"rep": layers[k]}, device_id_type=MESH,
        )

    def g_start(step, m):
        for way in range(2):
            @pl.when(g_sends(way, step))
            def _():
                g_copy(way, step, m).start()

    def g_land(step, m):
        for way in range(2):
            @pl.when(g_lands(way, step))
            def _():
                g_copy(way, step, m).wait_recv()

    def pack(k, m):
        part = jnp.dot(rz[k], gz[layers[k], :, hidden_at(m)], preferred_element_type=jnp.float32)
        ps[k, :, (c_me + m) % group] = part.astype(jnp.bfloat16).reshape(EXPERTS, CAP, half)
        for j in range(m, q, group):
            if j:
                p_copy(k, j).start()
        if m == 0:
            rb[k, me] = ps[k, e_me, c_me]

    def x_starts(step):
        for k in range(1, n):
            to = layers[k]
            @pl.when(((to > z) & (to == step)) | ((to < z) & (to == n - 1 - step)))
            def _():
                for c in range(group):
                    x_copy(k, c).start()

    def x_pack(k):
        for c in range(group):
            if k:
                x_copy(k, c).wait_recv()
            else:
                own_copy(c).wait()
            part = jnp.dot(rz[k], xz[k, c], preferred_element_type=jnp.float32)
            qs[k, :, c] = part.astype(jnp.bfloat16).reshape(EXPERTS, CAP, piece)
        for j in range(1, q):
            q_copy(k, j).start()
        xb[k, me] = qs[k, e_me, c_me]

    def x_turn(k):
        for j in range(1, q):
            q_copy(k, j).wait_recv()
        xt[:, k * rows : (k + 1) * rows] = xb[k].reshape(rows, piece).T

    def exchange(k):
        for j in range(1, q):
            p_copy(k, j).wait_recv()
        for m in range(1, group):
            h_copy(k, m).start()

    def tile_copy(m, at):
        start = pl.multiple_of((c_me + m) % group * half + at, 256)
        return pltpu.make_async_copy(
            wf.at[:, m * half + at : m * half + at + 256], wg_ref.at[:, pl.ds(start, 256)],
            tile_sem.at[(m * half + at) // 256],
        )

    def weight_rows(first, last):
        for m in range(group):
            for at in range(0, half, 256):
                total = None
                for k in range(first, last):
                    lhs = xt[:, k * rows : (k + 1) * rows]
                    if m == 0:
                        rhs = rb[k, :, :, at : at + 256]
                    else:
                        rhs = ph[m - 1, k, :, :, at : at + 256]
                    part = jnp.dot(lhs, rhs.reshape(rows, 256), preferred_element_type=jnp.float32)
                    total = part if total is None else total + part
                if first:
                    total = total + wf[:, m * half + at : m * half + at + 256]
                wf[:, m * half + at : m * half + at + 256] = total
                if last == n:
                    tile_copy(m, at).start()

    def grads_of(k, m):
        if m == 0:
            return rb[k].reshape(rows, half)
        return ph[m - 1, k].reshape(rows, half)

    def input_rows(k):
        total = None
        for m in range(group):
            if m:
                h_copy(k, m).wait_recv()
            part = lax.dot_general(
                grads_of(k, m), wb[:, hidden_at(m)], (((1,), (1,)), ((), ())),
                preferred_element_type=jnp.float32,
            )
            total = part if total is None else total + part
        db[k] = total.astype(jnp.bfloat16).reshape(q, CAP, piece)
        for j in range(1, q):
            b_copy(k, j).start()
        bk[k, c_me, e_me] = db[k, me]

    def unpack(k):
        for j in range(1, q):
            b_copy(k, j).wait_recv()
        for c in range(group):
            part = lax.dot_general(
                rz[k], bk[k, c].reshape(slots, piece), (((0,), (0,)), ((), ())),
                preferred_element_type=jnp.float32,
            )
            part = part.astype(jnp.bfloat16)
            if k:
                us[k, c] = part
            else:
                dx_ref[:, columns(c, z)] = part
        if k:
            u_copy(k).start()

    for m in range(group):
        g_start(0, m)
    for k in range(1, n):
        r_copy(k).start()
    for m in range(group):
        pack(0, m)
    x_pack(0)
    weights.wait()
    wb[...] = wf[...].astype(jnp.bfloat16)
    for k in range(1, n):
        r_copy(k).wait_recv()
        for m in range(group):
            g_land(k - 1, m)
            if k < n - 1:
                g_start(k, m)
            pack(k, m)
        x_starts(k)
        exchange(k - 1)
        if k >= 2:
            input_rows(k - 2)
        if k >= 3:
            unpack(k - 3)
    input_rows(n - 2)
    for k in range(max(n - 3, 0), n - 2):
        unpack(k)
    exchange(n - 1)
    x_pack(1)
    input_rows(n - 1)
    unpack(n - 2)
    for k in range(2, n - 1):
        x_pack(k)
    unpack(n - 1)
    if n > 2:
        x_pack(n - 1)
    for k in range(n // 2):
        x_turn(k)
    weight_rows(0, n // 2)
    for k in range(n // 2, n):
        x_turn(k)
    weight_rows(n // 2, n)
    for k in range(1, n):
        u_copy(k).wait_recv()
        for c in range(group):
            dx_ref[:, columns(c, layers[k])] = fin[k, c]
    for m in range(group):
        for at in range(0, half, 256):
            tile_copy(m, at).wait()

    for step in range(n - 1):
        for way in range(2):
            @pl.when(g_sends(way, step))
            def _():
                for m in range(group):
                    g_copy(way, step, m).wait_send()
    for k in range(n):
        if k:
            r_copy(k).wait_send()
            for c in range(group):
                x_copy(k, c).wait_send()
            u_copy(k).wait_send()
        for j in range(1, q):
            p_copy(k, j).wait_send()
            q_copy(k, j).wait_send()
            b_copy(k, j).wait_send()
        for m in range(1, group):
            h_copy(k, m).wait_send()


def tokens_move(
    activations,
    grad_hidden,
    pre_gate,
    pre_up,
    modality,
    expert_index,
    master,
    first_moment,
    second_moment,
):
    n = lax.axis_size("rep")
    q = lax.axis_size("exp")
    group = q // EXPERTS
    tok, width = activations.shape
    piece, hid2 = master.shape
    half = hid2 // group
    vmem = pl.BlockSpec(memory_space=pltpu.VMEM)
    anywhere = pl.BlockSpec(memory_space=pl.ANY)
    bf16 = jnp.bfloat16
    dma = pltpu.SemaphoreType.DMA
    input_grad, weight_grad = pl.pallas_call(
        rows_kernel,
        out_shape=(
            jax.ShapeDtypeStruct((tok, width), bf16),
            jax.ShapeDtypeStruct((piece, hid2), jnp.float32),
        ),
        in_specs=[anywhere, vmem, vmem, vmem, vmem, vmem, anywhere],
        out_specs=(vmem, anywhere),
        scratch_shapes=[
            pltpu.VMEM((n, tok, hid2), bf16),
            pltpu.VMEM((n, group, tok, piece), bf16),
            pltpu.VMEM((n, EXPERTS * CAP, tok), bf16),
            pltpu.VMEM((n, EXPERTS, group, CAP, half), bf16),
            pltpu.VMEM((n, q, CAP, half), bf16),
            pltpu.VMEM((n, EXPERTS, group, CAP, piece), bf16),
            pltpu.VMEM((n, q, CAP, piece), bf16),
            pltpu.VMEM((group - 1, n, q, CAP, half), bf16),
            pltpu.VMEM((piece, hid2), jnp.float32),
            pltpu.VMEM((piece, hid2), bf16),
            pltpu.VMEM((piece, n * q * CAP), bf16),
            pltpu.VMEM((n, q, CAP, piece), bf16),
            pltpu.VMEM((n, group, EXPERTS, CAP, piece), bf16),
            pltpu.VMEM((n, group, tok, piece), bf16),
            pltpu.VMEM((n, group, tok, piece), bf16),
            dma((2, n, group)), dma((2, n, group)),
            dma((n, group)), dma((n, group)),
            dma((n,)), dma((n,)),
            dma((n, q)), dma((n, q)),
            dma((n, q)), dma((n, q)),
            dma((n, group)), dma((n, group)),
            dma((n, q)), dma((n, q)),
            dma((n,)), dma((n,)),
            dma((group,)), dma((hid2 // 256,)),
            dma,
        ],
        compiler_params=pltpu.CompilerParams(
            collective_id=0, has_side_effects=True, vmem_limit_bytes=VMEM_GRANT
        ),
        name="rows_kernel",
    )(
        activations, grad_hidden, pre_gate, pre_up,
        modality.reshape(1, tok), expert_index.reshape(1, tok), master,
    )
    new_first = beta_one * first_moment + (1.0 - beta_one) * weight_grad
    new_second = beta_two * second_moment + (1.0 - beta_two) * weight_grad * weight_grad
    corr_one = 1.0 - beta_one**adam_count
    corr_two = 1.0 - beta_two**adam_count
    update = new_first / corr_one / (jnp.sqrt(new_second / corr_two) + adam_eps)
    new_master = master - learn_rate * update
    return (input_grad, new_master, new_first, new_second)


def body(*blocks):
    n = lax.axis_size("rep")
    q = lax.axis_size("exp")
    group = q // EXPERTS
    tok, width = blocks[0].shape
    piece, hid2 = blocks[6].shape
    held = n * q * CAP * (hid2 + 4 * piece) * 2 + 12 * piece * hid2
    held += n * tok * (hid2 + 3 * group * piece) * 2 + n * EXPERTS * CAP * group * hid2
    fits = held <= VMEM_GRANT * 3 // 4 and group >= 2 and n >= 2 and n & (n - 1) == 0
    if fits and piece % 128 == 0 and hid2 % 512 == 0 and hid2 // group % 256 == 0 and q * CAP % 128 == 0:
        return tokens_move(*blocks)
    return weights_move(*blocks)


def solution(mesh):
    in_specs = (
        P(("rep", "exp"), None),
        P(("rep", "exp"), None),
        P(("rep", "exp"), None),
        P(("rep", "exp"), None),
        P(("rep", "exp")),
        P(("rep", "exp")),
        P(("exp", "rep"), None),
        P(("exp", "rep"), None),
        P(("exp", "rep"), None),
    )
    out_specs = (
        P(("rep", "exp"), None),
        P(("exp", "rep"), None),
        P(("exp", "rep"), None),
        P(("exp", "rep"), None),
    )
    return jax.shard_map(body, mesh=mesh, in_specs=in_specs, out_specs=out_specs, check_vma=False)
```
